256 devices in a mesh: grp: 4 (over z_hi), ctx: 64 (over z_lo, x, y, core).
Axes of the slice: x: 4, y: 4, z: 8 (z_hi: 4, z_lo: 2; z = z_hi * 2 + z_lo), core: 2. Of those that a mesh axis runs over, the one named last changes fastest.
Arguments:
- queries: bfloat16 [4, 12288, 1024], P('grp', 'ctx'), may hold values from -160 to 160
- grad_out: bfloat16 [4, 12288, 1024], P('grp', 'ctx'), may hold values from -6 to 6
- rollout_cache: bfloat16 [4, 12288, 256], P('grp', 'ctx'), may hold values from -8 to 8
- prompt_cache: bfloat16 [4, 4096, 256], P('grp', 'ctx'), may hold values from -6 to 6
- rollout_hidden: bfloat16 [4, 12288, 5120], P('grp', 'ctx'), may hold values from -6 to 6
- prompt_hidden: bfloat16 [4, 4096, 5120], P('grp', 'ctx'), may hold values from -16 to 16
- lengths: int32 [4, 128], P('grp', 'ctx'), may hold values from 24 to 96, as said below
Outputs:
- query_grad: bfloat16 [4, 12288, 1024], P('grp', 'ctx')
- rollout_grad: bfloat16 [4, 12288, 256], P('grp', 'ctx')
- prompt_grad: bfloat16 [4, 4096, 256], P('grp', 'ctx')
- weight_grad: float32 [5120, 256], P('ctx')
The draws below stay inside these ranges and needn't reach their ends.
Inputs may be any that keep to these rules, and one draw needn't show every extreme that they name: `lengths`: in every group some rollout has exactly 96 tokens.
All inputs are finite; a program needn't handle non-finite values.
Results may differ from the reference program's by a relative error of at most 0.017.
Values may be sent and summed in bfloat16 or wider, within the bound.
A program may use at most 64 MiB of HBM per device.

```python
import math
import jax
import jax.numpy as jnp
from jax import lax

D = 5120
HDIM = 128
HEADS = 8
LMAX = 96
ROLL_DEV = 2
GROUPS = 4
PROMPT = 4096
CAP = 192
N_CTX = 64


def anchor_rows(key):
    prompt_keys = jax.random.normal(key, (GROUPS, PROMPT, HDIM), jnp.float32)
    return prompt_keys


def draw_prompt_cache(key, part):
    prompt_keys = anchor_rows(key)
    key = jax.random.fold_in(key, 1)
    values = jax.random.normal(jax.random.fold_in(key, 2), (GROUPS, PROMPT, HDIM), jnp.float32)
    return jnp.clip(jnp.concatenate([prompt_keys, values], axis=2), -6.0, 6.0).astype(jnp.bfloat16)


def draw_queries(key, part):
    key = jax.random.fold_in(key, 4)
    result = jax.random.normal(jax.random.fold_in(key, 5), (GROUPS, N_CTX * CAP, HEADS * HDIM), jnp.float32) * 2.0
    return jnp.clip(result, -160.0, 160.0).astype(jnp.bfloat16)


def draw_lengths(key, part):
    key = jax.random.fold_in(key, 8)
    drawn = jax.random.randint(jax.random.fold_in(key, 1), (GROUPS, N_CTX * ROLL_DEV), LMAX // 4, LMAX + 1)
    chosen = jax.random.randint(jax.random.fold_in(key, 2), (GROUPS, 1), 0, N_CTX * ROLL_DEV)
    places = lax.broadcasted_iota(jnp.int32, (GROUPS, N_CTX * ROLL_DEV), 1)
    return jnp.where(places == chosen, LMAX, drawn).astype(jnp.int32)


def raised(values, key, source, target, blocks, factor):
    def block_of(axis_at):
        return (jnp.arange(values.shape[axis_at]) // (values.shape[axis_at] // blocks)).reshape((-1,) + (1,) * (values.ndim - 1 - axis_at))

    near = jax.random.permutation(key, blocks)[block_of(target)]
    second = (block_of(target) + blocks // 2) % blocks
    return jnp.where((block_of(source) == near) | (block_of(source) == second), factor * values, values)


def block_scale(rng, extent, cuts, low, top_value):
    level, own = 1.0, jax.random.fold_in(rng, 6)
    for position, blocks in cuts:
        steps = jnp.exp(jax.random.uniform(jax.random.fold_in(own, position), (blocks,), jnp.float32, low / len(cuts), top_value / len(cuts)))
        level = level * jnp.repeat(steps, extent[position] // blocks).reshape([-1 if axis == position else 1 for axis in range(len(extent))])
    return level


def scatter_about(stream_key, dims, scale, bound, pieces=(), kind=jnp.bfloat16):
    factor_of = block_scale(stream_key, dims, pieces, -0.22, 0.18) if pieces else 1.0
    values = jax.random.normal(stream_key, dims, jnp.float32) * scale * factor_of
    return jnp.minimum(jnp.maximum(values, -bound), bound).astype(kind)


def heavy_noise(key, extent, spread, most, cuts, heavy, kind=jnp.bfloat16):
    entries = spread * jax.random.normal(key, extent, jnp.float32)
    if cuts:
        entries = entries * block_scale(key, extent, cuts, -0.22, 0.18)
    return jnp.clip(raised(entries, jax.random.fold_in(key, 3), *heavy), -most, most).astype(kind)


def setup_inputs(seed: int = 0) -> dict:
    arg_keys = jax.random.split(jax.random.key(seed), 8)
    queries = draw_queries(jax.random.fold_in(arg_keys[7], 71), 0)
    grad_out = scatter_about(arg_keys[1], (GROUPS, N_CTX * CAP, HEADS * HDIM), 1.0, 6.0, ((0, 4), (1, 64)))
    rollout_cache = scatter_about(arg_keys[2], (GROUPS, N_CTX * CAP, 2 * HDIM), 1.6, 8.0, ((0, 4), (1, 64)))
    prompt_cache = draw_prompt_cache(jax.random.fold_in(arg_keys[7], 71), 0)
    rollout_hidden = heavy_noise(arg_keys[4], (GROUPS, N_CTX * CAP, D), 1.0, 6.0, ((0, 4), (1, 64)), (0, 2, 4, 2.0))
    prompt_hidden = heavy_noise(arg_keys[5], (GROUPS, PROMPT, D), 1.0, 16.0, ((0, 4), (1, 64)), (1, 2, 64, 4.0))
    lengths = draw_lengths(jax.random.fold_in(arg_keys[7], 71), 0)
    return {"queries": queries, "grad_out": grad_out, "rollout_cache": rollout_cache, "prompt_cache": prompt_cache, "rollout_hidden": rollout_hidden, "prompt_hidden": prompt_hidden, "lengths": lengths}


def slot_grads(query_block, grad_block, cache_block, limit, prompt_keys, prompt_values):
    head_size = prompt_keys.shape[1]
    slot_len = query_block.shape[0]
    head_count = query_block.shape[1] // head_size
    scaling = 1.0 / math.sqrt(head_size)
    rows_query = query_block.reshape(slot_len, head_count, head_size).transpose(1, 0, 2).reshape(head_count * slot_len, head_size)
    rows_grad = grad_block.reshape(slot_len, head_count, head_size).transpose(1, 0, 2).reshape(head_count * slot_len, head_size)
    roll_keys = cache_block[:, :head_size]
    roll_values = cache_block[:, head_size:]
    prompt_scores = jnp.dot(rows_query, prompt_keys.T, preferred_element_type=jnp.float32) * scaling
    roll_scores = jnp.dot(rows_query, roll_keys.T, preferred_element_type=jnp.float32) * scaling
    query_pos = lax.broadcasted_iota(jnp.int32, (head_count, slot_len, slot_len), 1).reshape(head_count * slot_len, slot_len)
    key_pos = lax.broadcasted_iota(jnp.int32, (head_count, slot_len, slot_len), 2).reshape(head_count * slot_len, slot_len)
    allowed = (key_pos <= query_pos) & (key_pos < limit)
    live = (query_pos[:, 0] < limit).astype(jnp.float32)
    roll_scores = jnp.where(allowed, roll_scores, -1e+30)
    highest = jnp.maximum(lax.optimization_barrier(jnp.max(prompt_scores, axis=1)), lax.optimization_barrier(jnp.max(roll_scores, axis=1)))
    prompt_exp = jnp.exp(prompt_scores - highest[:, None])
    roll_exp = jnp.exp(roll_scores - highest[:, None])
    totals = lax.optimization_barrier(jnp.sum(prompt_exp, axis=1)) + lax.optimization_barrier(jnp.sum(roll_exp, axis=1))
    prompt_probs = prompt_exp / totals[:, None]
    roll_probs = roll_exp / totals[:, None]
    prompt_dp = jnp.dot(rows_grad, prompt_values.T, preferred_element_type=jnp.float32)
    roll_dp = jnp.dot(rows_grad, roll_values.T, preferred_element_type=jnp.float32)
    deltas = lax.optimization_barrier(jnp.sum(prompt_probs * prompt_dp, axis=1)) + lax.optimization_barrier(jnp.sum(roll_probs * roll_dp, axis=1))
    prompt_probs = prompt_probs * live[:, None]
    roll_probs = roll_probs * live[:, None]
    prompt_ds = (prompt_probs * (prompt_dp - deltas[:, None])).astype(jnp.bfloat16)
    roll_ds = (roll_probs * (roll_dp - deltas[:, None])).astype(jnp.bfloat16)
    prompt_pb = prompt_probs.astype(jnp.bfloat16)
    roll_pb = roll_probs.astype(jnp.bfloat16)
    dquery = (jnp.dot(prompt_ds, prompt_keys, preferred_element_type=jnp.float32) + jnp.dot(roll_ds, roll_keys, preferred_element_type=jnp.float32)) * scaling
    query_out = dquery.reshape(head_count, slot_len, head_size).transpose(1, 0, 2).reshape(slot_len, head_count * head_size).astype(jnp.bfloat16)
    prompt_terms = jnp.concatenate([jnp.dot(prompt_ds.T, rows_query, preferred_element_type=jnp.float32) * scaling, jnp.dot(prompt_pb.T, rows_grad, preferred_element_type=jnp.float32)], axis=1)
    roll_out = jnp.concatenate([jnp.dot(roll_ds.T, rows_query, preferred_element_type=jnp.float32) * scaling, jnp.dot(roll_pb.T, rows_grad, preferred_element_type=jnp.float32)], axis=1).astype(jnp.bfloat16)
    return (query_out, roll_out, prompt_terms)

def reference(queries, grad_out, rollout_cache, prompt_cache, rollout_hidden, prompt_hidden, lengths):
    head_size = prompt_cache.shape[2] // 2
    query_list = []
    rollout_list = []
    prompt_list = []
    weight_sum = jnp.zeros((prompt_hidden.shape[2], 2 * head_size), jnp.float32)
    indices = jnp.arange(N_CTX * ROLL_DEV, dtype=jnp.int32)
    for group in range(GROUPS):
        prompt_keys = prompt_cache[group][:, :head_size]
        prompt_values = prompt_cache[group][:, head_size:]
        group_queries = queries[group]
        group_grads = grad_out[group]
        group_cache = rollout_cache[group]
        group_lengths = lengths[group]

        def slot_step(carry, index):
            start = (index * LMAX).astype(jnp.int32)
            query_block = lax.dynamic_slice_in_dim(group_queries, start, LMAX, 0)
            grad_block = lax.dynamic_slice_in_dim(group_grads, start, LMAX, 0)
            cache_block = lax.dynamic_slice_in_dim(group_cache, start, LMAX, 0)
            query_out, roll_out, prompt_terms = slot_grads(query_block, grad_block, cache_block, group_lengths[index], prompt_keys, prompt_values)
            return (carry + prompt_terms, (query_out, roll_out))
        summed, (query_outs, roll_outs) = lax.scan(slot_step, jnp.zeros((PROMPT, 2 * head_size), jnp.float32), indices)
        query_group = query_outs.reshape(N_CTX * CAP, -1)
        roll_group = roll_outs.reshape(N_CTX * CAP, -1)
        prompt_group = summed.astype(jnp.bfloat16)
        weight_sum = weight_sum + jnp.dot(prompt_hidden[group].T, prompt_group, preferred_element_type=jnp.float32)
        weight_sum = weight_sum + jnp.dot(rollout_hidden[group].T, roll_group, preferred_element_type=jnp.float32)
        query_list.append(query_group)
        rollout_list.append(roll_group)
        prompt_list.append(prompt_group)
    return (jnp.stack(query_list), jnp.stack(rollout_list), jnp.stack(prompt_list), weight_sum)
```

```python
import math

import jax
import jax.numpy as jnp
from jax import lax
from jax.experimental import pallas as pl
from jax.experimental.pallas import tpu as pltpu
from jax.sharding import PartitionSpec as P

MESH = pl.DeviceIdType.MESH
F32, BF16 = jnp.float32, jnp.bfloat16
KEYS, ROLL, ROWS, HD = 4096, 192, 1536, 128
CHUNK, TILE = 512, 256
SCALE = 1.0 / math.sqrt(HD)


def dot(a, b):
    return jnp.dot(a, b, preferred_element_type=F32)


def dot_nt(a, b):
    return lax.dot_general(a, b, (((1,), (1,)), ((), ())), preferred_element_type=F32)


def dot_tn(a, b):
    return lax.dot_general(a, b, (((0,), (0,)), ((), ())), preferred_element_type=F32)


class Place:
    def __init__(self):
        self.g = lax.axis_index("grp")
        t = lax.axis_index("ctx")
        self.t = t
        self.c = lax.rem(t, 2)
        y = lax.rem(t // 2, 4)
        x = lax.rem(t // 8, 4)
        z = t // 32
        a = x + self.c * (y - x)
        self.b = y + self.c * (x - y)
        self.other_b = x + self.c * (y - x)
        self.s = a * 2 + z

    def dev(self, b, s):
        a, z = s // 2, lax.rem(s, 2)
        x = a + self.c * (b - a)
        y = b + self.c * (a - b)
        return (self.g, z * 32 + x * 8 + y * 2 + self.c)

    def core(self):
        return (self.g, self.t + 1 - 2 * self.c)

    def near(self, j):
        return self.dev(self.b, lax.rem(self.s + j, 8))

    def up(self):
        return self.dev(lax.rem(self.b + 1, 4), self.s)

    def down(self):
        return self.dev(lax.rem(self.b + 3, 4), self.s)

    def group(self, j):
        return (lax.rem(self.g + j, 4), self.t)

    def partners(self):
        return [self.core(), self.up(), self.down()] + [self.near(j) for j in range(1, 8)]


def barrier(devices):
    sem = pltpu.get_barrier_semaphore()
    for device in devices:
        pl.semaphore_signal(sem, inc=1, device_id=device, device_id_type=MESH)
    pl.semaphore_wait(sem, len(devices))


def remote(src, dst, send, recv, device):
    return pltpu.make_async_remote_copy(
        src_ref=src, dst_ref=dst, send_sem=send, recv_sem=recv, device_id=device, device_id_type=MESH
    )


def gather_kernel(cache_ref, kv, send, recv, recv_core):
    here = Place()
    base = here.c * 32
    copies = []

    def push(pos, sems, device, into):
        copy = remote(kv.at[pos], kv.at[pos], send.at[len(copies)], into, device)
        copy.start()
        copies.append(copy)

    def arrived(pos, sem):
        remote(kv.at[pos], kv.at[pos], send.at[0], sem, here.core()).wait_recv()

    def block(b, s):
        return lax.rem(here.b + b, 4) * 8 + s

    own = block(0, here.s)
    kv[base + own] = cache_ref[...]
    barrier(here.partners())
    for j in range(1, 8):
        push(base + own, None, here.near(j), recv.at[own])
    order = [lax.rem(here.s + 8 - i, 8) for i in range(8)]
    for i in range(8):
        at = block(0, order[i])
        if i:
            arrived(base + at, recv.at[at])
        push(base + at, None, here.up(), recv.at[at])
        push(base + at, None, here.down(), recv.at[at])
        push(base + at, None, here.core(), recv_core.at[at])
    for i in range(8):
        low, high = block(3, order[i]), block(1, order[i])
        arrived(base + low, recv.at[low])
        if i < 4:
            push(base + low, None, here.up(), recv.at[low])
        push(base + low, None, here.core(), recv_core.at[low])
        arrived(base + high, recv.at[high])
        if i >= 4:
            push(base + high, None, here.down(), recv.at[high])
        push(base + high, None, here.core(), recv_core.at[high])
    for i in range(8):
        at = block(2, order[i])
        arrived(base + at, recv.at[at])
        push(base + at, None, here.core(), recv_core.at[at])
    for at in range(32):
        arrived(32 - base + at, recv_core.at[at])
    for copy in copies:
        copy.wait_send()


def gather(cache):
    return pl.pallas_call(
        gather_kernel,
        out_shape=jax.ShapeDtypeStruct((64, 64, 256), BF16),
        in_specs=[pl.BlockSpec(memory_space=pltpu.VMEM)],
        out_specs=pl.BlockSpec(memory_space=pltpu.VMEM),
        scratch_shapes=[
            pltpu.SemaphoreType.DMA((63,)),
            pltpu.SemaphoreType.DMA((32,)),
            pltpu.SemaphoreType.DMA((32,)),
        ],
        compiler_params=pltpu.CompilerParams(collective_id=0, has_side_effects=True),
    )(cache)


def attention_kernel(len_ref, q_ref, g_ref, rc_ref, kv_ref, dq_ref, dr_ref, dp_ref, qa, ga, kt, S, DP, PB, DS):
    C = math.log2(math.e) * SCALE
    for h in range(8):
        qa[h * ROLL : (h + 1) * ROLL, :] = q_ref[:, h * HD : (h + 1) * HD]
        ga[h * ROLL : (h + 1) * ROLL, :] = g_ref[:, h * HD : (h + 1) * HD]
    for c in range(KEYS // CHUNK):
        kt[:, c * CHUNK : (c + 1) * CHUNK] = kv_ref[c * CHUNK : (c + 1) * CHUNK, :HD].T
    roll_kt = rc_ref[:, :HD].T
    n0, n1 = len_ref[0, 0], len_ref[0, 1]
    parts = [(c * CHUNK, CHUNK) for c in range(KEYS // CHUNK)] + [(KEYS, ROLL)]

    def fold(v, op):
        return op(v.reshape(v.shape[0] // 8, 8, TILE), axis=0)

    def tile(rt, _):
        r0 = pl.multiple_of(rt * TILE, TILE)
        q, g = qa[pl.ds(r0, TILE), :], ga[pl.ds(r0, TILE), :]
        rows = lax.broadcasted_iota(jnp.int32, (1, TILE), 1) + r0
        w = lax.rem(rows, ROLL)
        row_slot = (w >= 96).astype(jnp.int32)
        t = w - 96 * row_slot
        lim = jnp.where(row_slot == 1, n1, n0)
        live = (t < lim).astype(F32)
        keys = lax.broadcasted_iota(jnp.int32, (ROLL, 1), 0)
        key_slot = (keys >= 96).astype(jnp.int32)
        u = keys - 96 * key_slot
        ok = (key_slot == row_slot) & (u <= t) & (u < lim)
        s = jnp.where(ok, dot_nt(rc_ref[:, :HD], q), -1e30)
        S[KEYS:, :] = s
        top = fold(s, jnp.max)
        for at, size in parts[:-1]:
            s = dot_nt(kv_ref[at : at + size, :HD], q)
            S[at : at + size, :] = s
            top = jnp.maximum(top, fold(s, jnp.max))
        top = jnp.max(top, axis=0, keepdims=True) * C
        total = jnp.zeros((8, TILE), F32)
        weighted = jnp.zeros((8, TILE), F32)
        for at, size in parts:
            v = kv_ref[at : at + size, HD:] if at < KEYS else rc_ref[:, HD:]
            d = dot_nt(v, g)
            e = jnp.exp2(S[at : at + size, :] * C - top)
            S[at : at + size, :] = e
            DP[at : at + size, :] = d
            total = total + fold(e, jnp.sum)
            weighted = weighted + fold(e * d, jnp.sum)
        total = jnp.sum(total, axis=0, keepdims=True)
        delta = jnp.sum(weighted, axis=0, keepdims=True) / total
        inv = live / total
        acc = jnp.zeros((HD, TILE), F32)
        for at, size in parts:
            p = S[at : at + size, :] * inv
            ds = (p * (DP[at : at + size, :] - delta)).astype(BF16)
            PB[at : at + size, pl.ds(r0, TILE)] = p.astype(BF16)
            DS[at : at + size, pl.ds(r0, TILE)] = ds
            acc = acc + dot(kt[:, at : at + size] if at < KEYS else roll_kt, ds)
        dq_ref[pl.ds(r0, TILE), :] = (acc.T * SCALE).astype(BF16)
        return 0

    lax.fori_loop(0, ROWS // TILE, tile, 0)

    def grads(at):
        return jnp.concatenate([dot(DS[at, :], qa[...]) * SCALE, dot(PB[at, :], ga[...])], axis=1).astype(BF16)

    dr_ref[...] = grads(slice(KEYS, KEYS + ROLL))

    def key_tile(c, _):
        at = pl.ds(pl.multiple_of(c * TILE, TILE), TILE)
        dp_ref[at, :] = grads(at)
        return 0

    lax.fori_loop(0, KEYS // TILE, key_tile, 0)


def attention(lengths, q, g, cache, kv):
    vmem = pl.BlockSpec(memory_space=pltpu.VMEM)
    return pl.pallas_call(
        attention_kernel,
        out_shape=(
            jax.ShapeDtypeStruct((ROWS, HD), BF16),
            jax.ShapeDtypeStruct((ROLL, 2 * HD), BF16),
            jax.ShapeDtypeStruct((KEYS, 2 * HD), BF16),
        ),
        in_specs=[pl.BlockSpec(memory_space=pltpu.SMEM)] + [vmem] * 4,
        out_specs=(vmem,) * 3,
        scratch_shapes=[
            pltpu.VMEM((ROWS, HD), BF16),
            pltpu.VMEM((ROWS, HD), BF16),
            pltpu.VMEM((HD, KEYS), BF16),
            pltpu.VMEM((KEYS + ROLL, TILE), F32),
            pltpu.VMEM((KEYS + ROLL, TILE), F32),
            pltpu.VMEM((KEYS + ROLL, ROWS), BF16),
            pltpu.VMEM((KEYS + ROLL, ROWS), BF16),
        ],
        compiler_params=pltpu.CompilerParams(vmem_limit_bytes=60 << 20),
    )(lengths, q, g, cache, kv)


class Scatter:
    def __init__(self, here, buf, r0, ra, rb, r2a, r2b, r3, send, recv):
        self.here, self.buf, self.r0, self.ra, self.rb = here, buf, r0, ra, rb
        self.r2a, self.r2b, self.r3, self.send, self.recv = r2a, r2b, r3, send, recv
        self.copies = []

    def push(self, src, dst, sem, device):
        copy = remote(src, dst, self.send.at[len(self.copies)], self.recv.at[sem], device)
        copy.start()
        self.copies.append(copy)

    def got(self, dst, sem):
        remote(dst, dst, self.send.at[0], self.recv.at[sem], self.here.core()).wait_recv()

    def start(self):
        here = self.here
        for i, b in enumerate((2, 1, 3, 0)):
            at = lax.rem(here.other_b + b, 4) * 8
            self.push(self.buf.at[pl.ds(32 - here.c * 32 + at, 8)], self.r0.at[pl.ds(at, 8)], i, here.core())

    def finish(self):
        here = self.here
        base = here.c * 32

        def merge(i, b):
            at = lax.rem(here.b + b, 4) * 8
            self.got(self.r0.at[pl.ds(at, 8)], i)
            return at

        def add(at, k):
            total = self.buf[base + at + k].astype(F32) + self.r0[at + k].astype(F32)
            self.r0[at + k] = total.astype(BF16)

        far = merge(0, 2)
        for k in range(8):
            add(far, k)
        self.push(self.r0.at[pl.ds(far, 4)], self.ra, 4, here.up())
        self.push(self.r0.at[pl.ds(far + 4, 4)], self.rb, 5, here.down())
        up = merge(1, 1)
        for k in range(4, 8):
            add(up, k)
        self.push(self.r0.at[pl.ds(up + 4, 4)], self.r2a.at[pl.ds(4, 4)], 6, here.up())
        down = merge(2, 3)
        for k in range(4):
            add(down, k)
        self.push(self.r0.at[pl.ds(down, 4)], self.r2b.at[pl.ds(0, 4)], 7, here.down())
        self.got(self.ra, 4)
        for k in range(4):
            total = self.buf[base + up + k].astype(F32) + self.r0[up + k].astype(F32) + self.ra[k].astype(F32)
            self.r0[up + k] = total.astype(BF16)
        self.push(self.r0.at[pl.ds(up, 4)], self.r2a.at[pl.ds(0, 4)], 8, here.up())
        self.got(self.rb, 5)
        for k in range(4, 8):
            total = self.buf[base + down + k].astype(F32) + self.r0[down + k].astype(F32) + self.rb[k - 4].astype(F32)
            self.r0[down + k] = total.astype(BF16)
        self.push(self.r0.at[pl.ds(down + 4, 4)], self.r2b.at[pl.ds(4, 4)], 9, here.down())
        mine = merge(3, 0)
        self.got(self.r2a.at[pl.ds(4, 4)], 6)
        self.got(self.r2b.at[pl.ds(0, 4)], 7)
        self.got(self.r2a.at[pl.ds(0, 4)], 8)
        self.got(self.r2b.at[pl.ds(4, 4)], 9)

        def own(k):
            return (
                self.buf[base + mine + k].astype(F32)
                + self.r0[mine + k].astype(F32)
                + self.r2a[k].astype(F32)
                + self.r2b[k].astype(F32)
            )

        for j in range(1, 8):
            k = lax.rem(here.s + j, 8)
            self.r0[mine + k] = own(k).astype(BF16)
            self.push(self.r0.at[mine + k], self.r3.at[here.s], 10 + j, here.near(j))
        total = own(here.s)
        for j in range(1, 8):
            k = lax.rem(here.s + j, 8)
            self.got(self.r3.at[k], 10 + 8 - j)
            total = total + self.r3[k].astype(F32)
        return total

    def drain(self):
        for copy in self.copies:
            copy.wait_send()


def scatter_scratch(n):
    return [
        pltpu.VMEM((32, n, 256), BF16),
        pltpu.VMEM((4, n, 256), BF16),
        pltpu.VMEM((4, n, 256), BF16),
        pltpu.VMEM((8, n, 256), BF16),
        pltpu.VMEM((8, n, 256), BF16),
        pltpu.VMEM((8, n, 256), BF16),
        pltpu.SemaphoreType.DMA((17,)),
        pltpu.SemaphoreType.DMA((18,)),
    ]


def weight_kernel(dp_ref, dr_ref, hr_ref, hp_ref, pg_ref, w_ref, w1, wb, wg, gsend, grecv, *scratch):
    here = Place()
    prompt = Scatter(here, dp_ref, *scratch[:8])
    weight = Scatter(here, wb, *scratch[8:])
    barrier(here.partners() + [here.group(j) for j in range(1, 4)])
    prompt.start()
    for k in range(8):
        cols = slice(k * 640, (k + 1) * 640)
        w1[cols, :] = dot_tn(hr_ref[:, cols], dr_ref[...])
    own = prompt.finish().astype(BF16)
    pg_ref[...] = own
    for k in range(8):
        cols = slice(k * 640, (k + 1) * 640)
        part = (w1[cols, :] + dot_tn(hp_ref[:, cols], own)).astype(BF16)
        z, x = k // 4, k % 4
        for y in range(4):
            for c in range(2):
                a, b = (x, y) if c == 0 else (y, x)
                i = y * 2 + c
                wb[c * 32 + b * 8 + a * 2 + z] = part[i * 80 : (i + 1) * 80]
    weight.start()
    total = weight.finish()
    wg[0] = total.astype(BF16)
    copies = []
    for j in range(1, 4):
        copy = remote(wg.at[0], wg.at[4 - j], gsend.at[j], grecv.at[4 - j], here.group(j))
        copy.start()
        copies.append(copy)
    for j in range(1, 4):
        remote(wg.at[0], wg.at[j], gsend.at[j], grecv.at[j], here.group(j)).wait_recv()
        total = total + wg[j].astype(F32)
    w_ref[...] = total
    for copy in copies:
        copy.wait_send()
    prompt.drain()
    weight.drain()


def weights(dp, dr, hr, hp):
    vmem = pl.BlockSpec(memory_space=pltpu.VMEM)
    return pl.pallas_call(
        weight_kernel,
        out_shape=(jax.ShapeDtypeStruct((64, 256), BF16), jax.ShapeDtypeStruct((80, 256), F32)),
        in_specs=[vmem] * 4,
        out_specs=(vmem,) * 2,
        scratch_shapes=[
            pltpu.VMEM((5120, 256), F32),
            pltpu.VMEM((64, 80, 256), BF16),
            pltpu.VMEM((4, 80, 256), BF16),
            pltpu.SemaphoreType.DMA((4,)),
            pltpu.SemaphoreType.DMA((4,)),
        ]
        + scatter_scratch(64)
        + scatter_scratch(80),
        compiler_params=pltpu.CompilerParams(
            collective_id=1, has_side_effects=True, vmem_limit_bytes=56 << 20
        ),
    )(dp, dr, hr, hp)


def body(queries, grad_out, rollout_cache, prompt_cache, rollout_hidden, prompt_hidden, lengths):
    kv = gather(prompt_cache[0]).reshape(KEYS, 2 * HD)
    dq, dr, dp = attention(lengths, queries[0], grad_out[0], rollout_cache[0], kv)
    pg, w = weights(dp.reshape(64, 64, 256), dr, rollout_hidden[0], prompt_hidden[0])
    query_grad = dq.reshape(8, ROLL, HD).transpose(1, 0, 2).reshape(1, ROLL, 8 * HD)
    return (query_grad, dr[None], pg[None], w)


def solution(mesh):
    rows = P("grp", "ctx", None)
    in_specs = (rows,) * 6 + (P("grp", "ctx"),)
    out_specs = (rows, rows, rows, P("ctx", None))
    return jax.shard_map(body, mesh=mesh, in_specs=in_specs, out_specs=out_specs, check_vma=False)
```

```python
import math

import jax
import jax.numpy as jnp
from jax import lax
from jax.experimental import pallas as pl
from jax.experimental.pallas import tpu as pltpu
from jax.sharding import PartitionSpec as P

MESH = pl.DeviceIdType.MESH
F32, BF16 = jnp.float32, jnp.bfloat16
KEYS, ROLL, ROWS, HD, HEADS = 4096, 192, 1536, 128, 8
CHUNK, TILE = 256, 256
SCALE = 1.0 / math.sqrt(HD)
EXP_SCALE = math.log2(math.e) * SCALE


def dot(a, b):
    return jnp.dot(a, b, preferred_element_type=F32)


def dot_nt(a, b):
    return lax.dot_general(a, b, (((1,), (1,)), ((), ())), preferred_element_type=F32)


class Place:
    def __init__(self):
        self.g = lax.axis_index("grp")
        t = lax.axis_index("ctx")
        self.t = t
        self.c = lax.rem(t, 2)
        y = lax.rem(t // 2, 4)
        x = lax.rem(t // 8, 4)
        self.z = t // 32
        self.a = x + self.c * (y - x)
        self.b = y + self.c * (x - y)
        self.s = self.a * 2 + self.z

    def dev(self, a, b, z, core):
        x = a + self.c * (b - a)
        y = b + self.c * (a - b)
        return (self.g, z * 32 + x * 8 + y * 2 + core)

    def ring(self, i):
        return self.dev(self.a, lax.rem(self.b + i, 4), self.z, self.c)

    def near(self, j):
        s = lax.rem(self.s + j, 8)
        return self.dev(s // 2, self.b, lax.rem(s, 2), self.c)

    def cross_a(self, i):
        return self.dev(lax.rem(self.a + i, 4), self.b, self.z, 1 - self.c)

    def cross_b(self, i):
        return self.dev(self.a, lax.rem(self.b + i, 4), self.z, 1 - self.c)

    def group(self, j):
        return (lax.rem(self.g + j, 4), self.t)

    def partners(self):
        ring = [self.ring(i) for i in range(1, 4)]
        near = [self.near(j) for j in range(1, 8)]
        cross = [self.cross_a(i) for i in range(4)] + [self.cross_b(i) for i in range(1, 4)]
        return ring + near + cross + [self.group(j) for j in range(1, 4)]


def barrier(devices):
    sem = pltpu.get_barrier_semaphore()
    for device in devices:
        pl.semaphore_signal(sem, inc=1, device_id=device, device_id_type=MESH)
    pl.semaphore_wait(sem, len(devices))


class Net:
    def __init__(self, send, here):
        self.send, self.here, self.copies = send, here, []

    def copy(self, src, dst, sem, recv, device):
        return pltpu.make_async_remote_copy(
            src_ref=src, dst_ref=dst, send_sem=sem, recv_sem=recv, device_id=device, device_id_type=MESH
        )

    def push(self, src, dst, recv, device):
        copy = self.copy(src, dst, self.send.at[len(self.copies)], recv, device)
        copy.start()
        self.copies.append(copy)

    def got(self, dst, recv):
        self.copy(dst, dst, self.send.at[0], recv, self.here.cross_a(0)).wait_recv()

    def drain(self):
        for copy in self.copies:
            copy.wait_send()


SENDS = 63 + 7 + 7 + 7 + 17 + 7 + 3


def kernel(
    len_ref, q_ref, g_ref, rc_ref, cache_ref, hr_ref, hp_ref,
    dq_ref, dr_ref, pg_ref, w_ref,
    qa, ga, rc, hbuf, kv, kt, E, DP, PB, DS, dq, dp, ht, hx, grad, acc, wpart,
    r0, ra, rb, r2a, r2b, r3, wr3, wg,
    local, send, near_sem, core_sem, h_sem, gr_sem, gp_sem, s0_sem, s1_sem, s2_sem, w_sem, wg_sem,
):
    here = Place()
    net = Net(send, here)
    loads = []

    def load(src, dst):
        copy = pltpu.make_async_copy(src, dst, local.at[len(loads)])
        copy.start()
        loads.append(copy)

    load(cache_ref, kv.at[0])
    load(hr_ref, hbuf.at[pl.ds(0, ROLL)])
    load(hp_ref, hbuf.at[pl.ds(ROLL, 64)])
    load(rc_ref, rc)
    for h in range(HEADS):
        rows, cols = pl.ds(h * ROLL, ROLL), pl.ds(h * HD, HD)
        load(q_ref.at[:, cols], qa.at[rows])
        load(g_ref.at[:, cols], ga.at[rows])
    barrier(here.partners())

    loads[0].wait()
    core = here.cross_a(0)
    up, down = here.ring(1), here.ring(3)
    for j in range(1, 8):
        net.push(kv.at[0], kv.at[8 - j], near_sem.at[8 - j], here.near(j))

    def spread(j):
        net.push(kv.at[j], kv.at[24 + j], near_sem.at[24 + j], up)
        net.push(kv.at[j], kv.at[8 + j], near_sem.at[8 + j], down)
        net.push(kv.at[j], kv.at[32 + j], core_sem.at[j], core)

    def arrived(k):
        net.got(kv.at[k], near_sem.at[k])

    def to_core(k):
        net.push(kv.at[k], kv.at[32 + k], core_sem.at[k], core)

    spread(0)
    for j in range(1, 8):
        arrived(j)
        spread(j)

    loads[1].wait()
    loads[2].wait()
    for k in range(8):
        z, x = k // 4, k % 4
        part = hbuf[:, k * 640 : (k + 1) * 640].T.reshape(4, 2, 80, 256)
        for y in range(4):
            ht[0, y, z, x] = part[y, 0]
            ht[1, x, z, y] = part[y, 1]
        if k < 8:
            arrived(24 + k)
            if k < 4:
                net.push(kv.at[24 + k], kv.at[16 + k], near_sem.at[16 + k], up)
            to_core(24 + k)
            arrived(8 + k)
            if k >= 4:
                net.push(kv.at[8 + k], kv.at[16 + k], near_sem.at[16 + k], down)
            to_core(8 + k)
    for k in range(16, 24):
        arrived(k)
        to_core(k)
    for i in range(1, 4):
        net.push(ht.at[here.c, lax.rem(here.b + i, 4)], hx.at[4 - i], h_sem.at[4 - i], here.ring(i))
    for i in range(4):
        slot = 4 + (4 - i) % 4
        net.push(ht.at[1 - here.c, lax.rem(here.a + i, 4)], hx.at[slot], h_sem.at[slot], here.cross_a(i))
    for k in range(32):
        net.got(kv.at[32 + k], core_sem.at[k])
    for copy in loads[3:]:
        copy.wait()

    def keys(at, size):
        return kv[at // 64 : (at + size) // 64, :, :HD].reshape(size, HD)

    def values(at, size):
        return kv[at // 64 : (at + size) // 64, :, HD:].reshape(size, HD)

    for c in range(8):
        kt[:, c * 512 : (c + 1) * 512] = keys(c * 512, 512).T
    roll_kt = rc[:, :HD].T
    n0, n1 = len_ref[0, 0], len_ref[0, 1]
    parts = [(c * CHUNK, CHUNK) for c in range(KEYS // CHUNK)] + [(KEYS, ROLL)]
    for r0_ in range(0, ROWS, TILE):
        q, g = qa[r0_ : r0_ + TILE, :], ga[r0_ : r0_ + TILE, :]
        rows = lax.broadcasted_iota(jnp.int32, (1, TILE), 1) + r0_
        w = lax.rem(rows, ROLL)
        row_slot = (w >= 96).astype(jnp.int32)
        t = w - 96 * row_slot
        lim = jnp.where(row_slot == 1, n1, n0)
        live = (t < lim).astype(F32)
        idx = lax.broadcasted_iota(jnp.int32, (ROLL, 1), 0)
        key_slot = (idx >= 96).astype(jnp.int32)
        u = idx - 96 * key_slot
        ok = (key_slot == row_slot) & (u <= t) & (u < lim)
        top = jnp.full((8, TILE), -1e30, F32)
        total = jnp.zeros((8, TILE), F32)
        weighted = jnp.zeros((8, TILE), F32)
        tops = []
        for at, n in parts:
            if at < KEYS:
                s = dot_nt(keys(at, n), q) * EXP_SCALE
                d = dot_nt(values(at, n), g)
            else:
                s = jnp.where(ok, dot_nt(rc[:, :HD], q) * EXP_SCALE, -1e30)
                d = dot_nt(rc[:, HD:], g)
            s = s.reshape(n // 8, 8, TILE)
            newest = jnp.maximum(top, jnp.max(s, axis=0))
            shrink = jnp.exp2(top - newest)
            top = newest
            e = jnp.exp2(s - top[None])
            E[at : at + n, :] = e.reshape(n, TILE)
            DP[at : at + n, :] = d
            total = total * shrink + jnp.sum(e, axis=0)
            weighted = weighted * shrink + jnp.sum(e * d.reshape(n // 8, 8, TILE), axis=0)
            tops.append(top)
        highest = jnp.max(top, axis=0, keepdims=True)
        last = jnp.exp2(top - highest)
        sums = jnp.sum(total * last, axis=0, keepdims=True)
        delta = jnp.broadcast_to(jnp.sum(weighted * last, axis=0, keepdims=True) / sums, (8, TILE))
        inv = live / sums
        turned = jnp.zeros((HD, TILE), F32)
        for (at, n), old in zip(parts, tops):
            factor = jnp.exp2(old - highest) * inv
            p = E[at : at + n, :].reshape(n // 8, 8, TILE) * factor[None]
            ds = (p * (DP[at : at + n, :].reshape(n // 8, 8, TILE) - delta[None])).reshape(n, TILE).astype(BF16)
            PB[at : at + n, r0_ : r0_ + TILE] = p.reshape(n, TILE).astype(BF16)
            DS[at : at + n, r0_ : r0_ + TILE] = ds
            turned = turned + dot(kt[:, at : at + n] if at < KEYS else roll_kt, ds)
        dq[r0_ : r0_ + TILE, :] = (turned.T * SCALE).astype(BF16)
    stores = []
    for h in range(HEADS):
        rows, cols = pl.ds(h * ROLL, ROLL), pl.ds(h * HD, HD)
        copy = pltpu.make_async_copy(dq.at[rows], dq_ref.at[:, cols], local.at[len(loads) + h])
        copy.start()
        stores.append(copy)

    def grads(at, n):
        both = [dot(DS[at : at + n, :], qa[...]) * SCALE, dot(PB[at : at + n, :], ga[...])]
        return jnp.concatenate(both, axis=1).astype(BF16)

    def share(src, dst, sems):
        for i in range(1, 4):
            net.push(src(0), dst(4 - i), sems.at[4 - i], here.ring(i))
        for i in range(4):
            slot = 4 + (4 - i) % 4
            net.push(src(0), dst(slot), sems.at[slot], here.cross_a(i))

    def roll_part(k):
        return grad.at[k, pl.ds(0, ROLL)]

    def prompt_part(k):
        return grad.at[k, pl.ds(ROLL, 64)]

    mine = grads(KEYS, ROLL)
    dr_ref[...] = mine
    grad[0, :ROLL] = mine
    share(roll_part, roll_part, gr_sem)

    def block(k):
        dp[k * 8 : (k + 1) * 8] = grads(k * 512, 512).reshape(8, 64, 256)

    for i, b in enumerate((2, 1, 3, 0)):
        block(4 + b)
        net.push(dp.at[pl.ds(32 + b * 8, 8)], r0.at[pl.ds(b * 8, 8)], s0_sem.at[b], core)

    def merge(at, n, extra=None):
        total = dp[at : at + n].astype(F32) + r0[at : at + n].astype(F32)
        if extra is not None:
            total = total + extra[...].astype(F32)
        r0[at : at + n] = total.astype(BF16)

    def got_core(b):
        net.got(r0.at[pl.ds(b * 8, 8)], s0_sem.at[b])

    block(2)
    got_core(2)
    merge(16, 8)
    net.push(r0.at[pl.ds(16, 4)], ra, s1_sem.at[0], up)
    net.push(r0.at[pl.ds(20, 4)], rb, s1_sem.at[1], down)
    block(1)
    got_core(1)
    merge(12, 4)
    net.push(r0.at[pl.ds(12, 4)], r2a.at[pl.ds(4, 4)], s1_sem.at[2], up)
    block(3)
    got_core(3)
    merge(24, 4)
    net.push(r0.at[pl.ds(24, 4)], r2b.at[pl.ds(0, 4)], s1_sem.at[3], down)
    block(0)
    net.got(ra, s1_sem.at[0])
    merge(8, 4, ra)
    net.push(r0.at[pl.ds(8, 4)], r2a.at[pl.ds(0, 4)], s1_sem.at[4], up)
    net.got(rb, s1_sem.at[1])
    merge(28, 4, rb)
    net.push(r0.at[pl.ds(28, 4)], r2b.at[pl.ds(4, 4)], s1_sem.at[5], down)
    got_core(0)
    net.got(r2a.at[pl.ds(4, 4)], s1_sem.at[2])
    net.got(r2b.at[pl.ds(0, 4)], s1_sem.at[3])
    net.got(r2a.at[pl.ds(0, 4)], s1_sem.at[4])
    net.got(r2b.at[pl.ds(4, 4)], s1_sem.at[5])

    def own(k):
        return dp[k].astype(F32) + r0[k].astype(F32) + r2a[k].astype(F32) + r2b[k].astype(F32)

    for j in range(1, 8):
        r0[j] = own(j).astype(BF16)
        net.push(r0.at[j], r3.at[8 - j], s2_sem.at[8 - j], here.near(j))
    prompt = own(0)
    for j in range(1, 8):
        net.got(r3.at[j], s2_sem.at[j])
        prompt = prompt + r3[j].astype(F32)
    pg_ref[...] = prompt.astype(BF16)
    grad[0, ROLL:] = prompt.astype(BF16)
    share(prompt_part, prompt_part, gp_sem)

    part = dot(ht[here.c, here.b].reshape(640, 256), grad[0])
    for k in range(1, 8):
        net.got(hx.at[k], h_sem.at[k])
        net.got(roll_part(k), gr_sem.at[k])
        net.got(prompt_part(k), gp_sem.at[k])
        part = part + dot(hx[k].reshape(640, 256), grad[k])
    acc[...] = part.reshape(2, 4, 80, 256)
    wpart[...] = part.astype(BF16).reshape(2, 4, 80, 256)
    for j in range(1, 8):
        s = lax.rem(here.s + j, 8)
        net.push(wpart.at[lax.rem(s, 2), s // 2], wr3.at[8 - j], w_sem.at[8 - j], here.near(j))
    total = acc[here.z, here.a]
    for j in range(1, 8):
        net.got(wr3.at[j], w_sem.at[j])
        total = total + wr3[j].astype(F32)
    wg[0] = total.astype(BF16)
    for j in range(1, 4):
        net.push(wg.at[0], wg.at[4 - j], wg_sem.at[4 - j], here.group(j))
    for j in range(1, 4):
        net.got(wg.at[j], wg_sem.at[j])
        total = total + wg[j].astype(F32)
    w_ref[...] = total
    for copy in stores:
        copy.wait()
    net.drain()


def whole(lengths, q, g, rc, cache, hr, hp):
    vmem, hbm = pl.BlockSpec(memory_space=pltpu.VMEM), pl.BlockSpec(memory_space=pl.ANY)
    dma = pltpu.SemaphoreType.DMA

    def buf(*shape, kind=BF16):
        return pltpu.VMEM(shape, kind)

    scratch = [
        buf(ROWS, HD), buf(ROWS, HD), buf(ROLL, 2 * HD), buf(256, 5120),
        buf(64, 64, 256), buf(HD, KEYS),
        buf(KEYS + ROLL, TILE, kind=F32), buf(KEYS + ROLL, TILE, kind=F32),
        buf(KEYS + ROLL, ROWS), buf(KEYS + ROLL, ROWS),
        buf(ROWS, HD), buf(64, 64, 256),
        buf(2, 4, 2, 4, 80, 256), buf(8, 2, 4, 80, 256), buf(8, 256, 256),
        buf(2, 4, 80, 256, kind=F32), buf(2, 4, 80, 256),
        buf(32, 64, 256), buf(4, 64, 256), buf(4, 64, 256),
        buf(8, 64, 256), buf(8, 64, 256), buf(8, 64, 256),
        buf(8, 80, 256), buf(4, 80, 256),
        dma((28,)), dma((SENDS,)), dma((32,)), dma((32,)), dma((8,)), dma((8,)), dma((8,)),
        dma((4,)), dma((6,)), dma((8,)), dma((8,)), dma((4,)),
    ]
    return pl.pallas_call(
        kernel,
        out_shape=(
            jax.ShapeDtypeStruct((ROLL, HEADS * HD), BF16),
            jax.ShapeDtypeStruct((ROLL, 2 * HD), BF16),
            jax.ShapeDtypeStruct((64, 2 * HD), BF16),
            jax.ShapeDtypeStruct((80, 2 * HD), F32),
        ),
        in_specs=[pl.BlockSpec(memory_space=pltpu.SMEM)] + [hbm] * 6,
        out_specs=(hbm, vmem, vmem, vmem),
        scratch_shapes=scratch,
        compiler_params=pltpu.CompilerParams(
            collective_id=0, has_side_effects=True, vmem_limit_bytes=62 << 20
        ),
    )(lengths, q, g, rc, cache, hr, hp)


def finish_kernel(*refs):
    ins, outs, sems = refs[:4], refs[4:8], refs[8]
    copies = [pltpu.make_async_copy(a, b, sems.at[i]) for i, (a, b) in enumerate(zip(ins, outs))]
    for copy in copies:
        copy.start()
    for copy in copies:
        copy.wait()


def finish(arrays):
    hbm = pl.BlockSpec(memory_space=pl.ANY)
    return pl.pallas_call(
        finish_kernel,
        out_shape=tuple(jax.ShapeDtypeStruct(a.shape, a.dtype) for a in arrays),
        in_specs=[hbm] * 4,
        out_specs=(hbm,) * 4,
        scratch_shapes=[pltpu.SemaphoreType.DMA((4,))],
    )(*arrays)


def body(queries, grad_out, rollout_cache, prompt_cache, rollout_hidden, prompt_hidden, lengths):
    outs = whole(
        lengths, queries[0], grad_out[0], rollout_cache[0], prompt_cache[0], rollout_hidden[0], prompt_hidden[0]
    )
    dq, dr, pg, w = finish(outs)
    return (dq[None], dr[None], pg[None], w)


def solution(mesh):
    rows = P("grp", "ctx", None)
    in_specs = (rows,) * 6 + (P("grp", "ctx"),)
    out_specs = (rows, rows, rows, P("ctx", None))
    return jax.shard_map(body, mesh=mesh, in_specs=in_specs, out_specs=out_specs, check_vma=False)
```

```python
import math

import jax
import jax.numpy as jnp
from jax import lax
from jax.experimental import pallas as pl
from jax.experimental.pallas import tpu as pltpu
from jax.sharding import PartitionSpec as P

MESH = pl.DeviceIdType.MESH
F32, BF16 = jnp.float32, jnp.bfloat16
KEYS, ROLL, ROWS, HD, HEADS = 4096, 192, 1536, 128, 8
CHUNK, TILE = 256, 256
SCALE = 1.0 / math.sqrt(HD)
EXP_SCALE = math.log2(math.e) * SCALE


def dot(a, b):
    return jnp.dot(a, b, preferred_element_type=F32)


def dot_nt(a, b):
    return lax.dot_general(a, b, (((1,), (1,)), ((), ())), preferred_element_type=F32)


class Place:
    def __init__(self):
        self.g = lax.axis_index("grp")
        t = lax.axis_index("ctx")
        self.t = t
        self.c = lax.rem(t, 2)
        y = lax.rem(t // 2, 4)
        x = lax.rem(t // 8, 4)
        self.z = t // 32
        self.a = x + self.c * (y - x)
        self.b = y + self.c * (x - y)
        self.s = self.a * 2 + self.z

    def dev(self, a, b, z, core):
        x = a + self.c * (b - a)
        y = b + self.c * (a - b)
        return (self.g, z * 32 + x * 8 + y * 2 + core)

    def ring(self, i):
        return self.dev(self.a, lax.rem(self.b + i, 4), self.z, self.c)

    def near(self, j):
        s = lax.rem(self.s + j, 8)
        return self.dev(s // 2, self.b, lax.rem(s, 2), self.c)

    def cross_a(self, i):
        return self.dev(lax.rem(self.a + i, 4), self.b, self.z, 1 - self.c)

    def cross_b(self, i):
        return self.dev(self.a, lax.rem(self.b + i, 4), self.z, 1 - self.c)

    def group(self, j):
        return (lax.rem(self.g + j, 4), self.t)

    def partners(self):
        ring = [self.ring(i) for i in range(1, 4)]
        near = [self.near(j) for j in range(1, 8)]
        cross = [self.cross_a(i) for i in range(4)] + [self.cross_b(i) for i in range(1, 4)]
        return ring + near + cross + [self.group(j) for j in range(1, 4)]


def greet(devices):
    for device in devices:
        pl.semaphore_signal(pltpu.get_barrier_semaphore(), inc=1, device_id=device, device_id_type=MESH)


class Net:
    def __init__(self, send, here):
        self.send, self.here, self.copies = send, here, []

    def copy(self, src, dst, sem, recv, device):
        return pltpu.make_async_remote_copy(
            src_ref=src, dst_ref=dst, send_sem=sem, recv_sem=recv, device_id=device, device_id_type=MESH
        )

    def push(self, src, dst, recv, device):
        copy = self.copy(src, dst, self.send.at[len(self.copies)], recv, device)
        copy.start()
        self.copies.append(copy)

    def got(self, dst, recv):
        self.copy(dst, dst, self.send.at[0], recv, self.here.cross_a(0)).wait_recv()

    def drain(self):
        for copy in self.copies:
            copy.wait_send()


SENDS = 63 + 7 + 7 + 7 + 17 + 7 + 3


def kernel(
    len_ref, q_ref, g_ref, rc_ref, cache_ref, hr_ref, hp_ref,
    dq_ref, dr_ref, pg_ref, w_ref,
    qa, ga, rc, hbuf, kv, kt, E, DP, PB, DS, dq, ht, hx, grad, gp, acc, wpart,
    r0, ra, rb, r3, wr3, wg,
    local, send, near_sem, core_sem, h_sem, gr_sem, gp_sem, s0_sem, s1_sem, s2_sem, w_sem, wg_sem,
):
    here = Place()
    net = Net(send, here)
    dp, r2a, r2b = hbuf, hbuf.at[:, pl.ds(KEYS, 512)], hbuf.at[:, pl.ds(KEYS + 512, 512)]
    loads = []

    def load(src, dst):
        copy = pltpu.make_async_copy(src, dst, local.at[len(loads)])
        copy.start()
        loads.append(copy)

    load(cache_ref, kv.at[0])
    load(hr_ref, hbuf.at[pl.ds(0, ROLL)])
    load(hp_ref, hbuf.at[pl.ds(ROLL, 64)])
    load(rc_ref, rc)
    for h in range(HEADS):
        rows, cols = pl.ds(h * ROLL, ROLL), pl.ds(h * HD, HD)
        load(q_ref.at[:, cols], qa.at[rows])
        load(g_ref.at[:, cols], ga.at[rows])
    partners = here.partners()
    greet(partners)

    grad[:, ROLL:] = jnp.zeros((8, 64, 256), BF16)
    gp[:, :64] = jnp.zeros((8, 64, 256), BF16)
    loads[1].wait()
    loads[2].wait()
    for k in range(8):
        z, x = k // 4, k % 4
        part = hbuf[:, k * 640 : (k + 1) * 640].T.reshape(4, 2, 80, 256)
        for y in range(4):
            ht[0, y, z, x] = part[y, 0]
            ht[1, x, z, y] = part[y, 1]
    pl.semaphore_wait(pltpu.get_barrier_semaphore(), len(partners))

    loads[0].wait()
    core = here.cross_a(0)
    up, down = here.ring(1), here.ring(3)
    for j in range(1, 8):
        net.push(kv.at[0], kv.at[8 - j], near_sem.at[8 - j], here.near(j))

    def spread(j):
        net.push(kv.at[j], kv.at[24 + j], near_sem.at[24 + j], up)
        net.push(kv.at[j], kv.at[8 + j], near_sem.at[8 + j], down)
        net.push(kv.at[j], kv.at[32 + j], core_sem.at[j], core)

    def arrived(k):
        net.got(kv.at[k], near_sem.at[k])

    def to_core(k):
        net.push(kv.at[k], kv.at[32 + k], core_sem.at[k], core)

    spread(0)
    for j in range(1, 8):
        arrived(j)
        spread(j)

    for k in range(8):
        arrived(24 + k)
        if k < 4:
            net.push(kv.at[24 + k], kv.at[16 + k], near_sem.at[16 + k], up)
        to_core(24 + k)
        arrived(8 + k)
        if k >= 4:
            net.push(kv.at[8 + k], kv.at[16 + k], near_sem.at[16 + k], down)
        to_core(8 + k)
    for k in range(16, 24):
        arrived(k)
        to_core(k)
    for i in range(1, 4):
        net.push(ht.at[here.c, lax.rem(here.b + i, 4)], hx.at[3 - i], h_sem.at[4 - i], here.ring(i))
    for i in range(4):
        slot = 4 + (4 - i) % 4
        net.push(ht.at[1 - here.c, lax.rem(here.a + i, 4)], hx.at[slot - 1], h_sem.at[slot], here.cross_a(i))
    for k in range(32):
        net.got(kv.at[32 + k], core_sem.at[k])
    for copy in loads[3:]:
        copy.wait()

    def keys(at, size):
        return kv[at // 64 : (at + size) // 64, :, :HD].reshape(size, HD)

    def values(at, size):
        return kv[at // 64 : (at + size) // 64, :, HD:].reshape(size, HD)

    for c in range(8):
        kt[:, c * 512 : (c + 1) * 512] = keys(c * 512, 512).T
    roll_kt = rc[:, :HD].T
    n0, n1 = len_ref[0, 0], len_ref[0, 1]
    parts = [(c * CHUNK, CHUNK) for c in range(KEYS // CHUNK)] + [(KEYS, ROLL)]
    for r0_ in range(0, ROWS, TILE):
        q, g = qa[r0_ : r0_ + TILE, :], ga[r0_ : r0_ + TILE, :]
        rows = lax.broadcasted_iota(jnp.int32, (1, TILE), 1) + r0_
        w = lax.rem(rows, ROLL)
        row_slot = (w >= 96).astype(jnp.int32)
        t = w - 96 * row_slot
        lim = jnp.where(row_slot == 1, n1, n0)
        live = (t < lim).astype(F32)
        idx = lax.broadcasted_iota(jnp.int32, (ROLL, 1), 0)
        key_slot = (idx >= 96).astype(jnp.int32)
        u = idx - 96 * key_slot
        ok = (key_slot == row_slot) & (u <= t) & (u < lim)
        top = jnp.full((8, TILE), -1e30, F32)
        total = jnp.zeros((8, TILE), F32)
        weighted = jnp.zeros((8, TILE), F32)
        tops = []
        for at, n in parts:
            if at < KEYS:
                s = dot_nt(keys(at, n), q) * EXP_SCALE
                d = dot_nt(values(at, n), g)
            else:
                s = jnp.where(ok, dot_nt(rc[:, :HD], q) * EXP_SCALE, -1e30)
                d = dot_nt(rc[:, HD:], g)
            s = s.reshape(n // 8, 8, TILE)
            newest = jnp.maximum(top, jnp.max(s, axis=0))
            shrink = jnp.exp2(top - newest)
            top = newest
            e = jnp.exp2(s - top[None])
            E[at : at + n, :] = e.reshape(n, TILE)
            DP[at : at + n, :] = d
            total = total * shrink + jnp.sum(e, axis=0)
            weighted = weighted * shrink + jnp.sum(e * d.reshape(n // 8, 8, TILE), axis=0)
            tops.append(top)
        highest = jnp.max(top, axis=0, keepdims=True)
        last = jnp.exp2(top - highest)
        sums = jnp.sum(total * last, axis=0, keepdims=True)
        delta = jnp.broadcast_to(jnp.sum(weighted * last, axis=0, keepdims=True) / sums, (8, TILE))
        inv = live / sums
        for (at, n), old in zip(parts, tops):
            factor = jnp.exp2(old - highest) * inv
            p = E[at : at + n, :].reshape(n // 8, 8, TILE) * factor[None]
            ds = (p * (DP[at : at + n, :].reshape(n // 8, 8, TILE) - delta[None])).reshape(n, TILE).astype(BF16)
            PB[at : at + n, r0_ : r0_ + TILE] = p.reshape(n, TILE).astype(BF16)
            DS[at : at + n, r0_ : r0_ + TILE] = ds

    def query_part(i):
        cols = slice(i * TILE, (i + 1) * TILE)
        turned = dot(kt[...], DS[:KEYS, cols]) + dot(roll_kt, DS[KEYS:, cols])
        dq[cols, :] = (turned.T * SCALE).astype(BF16)

    def grads(at, n):
        both = [dot(DS[at : at + n, :], qa[...]) * SCALE, dot(PB[at : at + n, :], ga[...])]
        return jnp.concatenate(both, axis=1).astype(BF16)

    def share(src, dst, sems):
        for i in range(1, 4):
            net.push(src(0), dst(4 - i), sems.at[4 - i], here.ring(i))
        for i in range(4):
            slot = 4 + (4 - i) % 4
            net.push(src(0), dst(slot), sems.at[slot], here.cross_a(i))

    def roll_part(k):
        return grad.at[k, pl.ds(0, ROLL)]

    def prompt_part(k):
        return gp.at[k, pl.ds(64, 64)]

    mine = grads(KEYS, ROLL)
    dr_ref[...] = mine
    grad[0, :ROLL] = mine
    share(roll_part, roll_part, gr_sem)

    def cell(ref, k):
        return ref.at[pl.ds(k % 4 * 64, 64), pl.ds(k // 4 * 256, 256)]

    def cells(ref, k, n):
        return ref.at[:, pl.ds(k // 4 * 256, n // 4 * 256)]

    def block(k):
        new = grads(k * 512, 512)
        cells(dp, k * 8, 4)[...] = new[:256]
        cells(dp, k * 8 + 4, 4)[...] = new[256:]

    def other(b):
        block(4 + b)
        net.push(cells(dp, 32 + b * 8, 8), cells(r0, b * 8, 8), s0_sem.at[b], core)

    def merge(at, n, extra=None):
        total = cells(dp, at, n)[...].astype(F32) + cells(r0, at, n)[...].astype(F32)
        if extra is not None:
            total = total + extra[...].astype(F32)
        cells(r0, at, n)[...] = total.astype(BF16)

    def got_core(b):
        net.got(cells(r0, b * 8, 8), s0_sem.at[b])

    other(2)
    block(2)
    other(1)
    got_core(2)
    merge(16, 8)
    net.push(cells(r0, 16, 4), ra, s1_sem.at[0], up)
    net.push(cells(r0, 20, 4), rb, s1_sem.at[1], down)
    other(3)
    block(1)
    got_core(1)
    merge(12, 4)
    net.push(cells(r0, 12, 4), cells(r2a, 4, 4), s1_sem.at[2], up)
    block(3)
    got_core(3)
    merge(24, 4)
    net.push(cells(r0, 24, 4), cells(r2b, 0, 4), s1_sem.at[3], down)
    other(0)
    net.got(ra, s1_sem.at[0])
    merge(8, 4, ra)
    net.push(cells(r0, 8, 4), cells(r2a, 0, 4), s1_sem.at[4], up)
    net.got(rb, s1_sem.at[1])
    merge(28, 4, rb)
    net.push(cells(r0, 28, 4), cells(r2b, 4, 4), s1_sem.at[5], down)
    block(0)
    query_part(0)
    got_core(0)
    net.got(cells(r2a, 4, 4), s1_sem.at[2])
    net.got(cells(r2b, 0, 4), s1_sem.at[3])
    net.got(cells(r2a, 0, 4), s1_sem.at[4])
    net.got(cells(r2b, 4, 4), s1_sem.at[5])

    def own(k):
        return sum(cell(ref, k)[...].astype(F32) for ref in (dp, r0, r2a, r2b))

    for j in range(1, 8):
        cell(r0, j)[...] = own(j).astype(BF16)
        net.push(cell(r0, j), r3.at[8 - j], s2_sem.at[8 - j], here.near(j))
    prompt = own(0)
    query_part(1)
    query_part(2)
    for k in range(1, 8):
        net.got(hx.at[k - 1], h_sem.at[k])
        net.got(roll_part(k), gr_sem.at[k])
    part = dot(ht[here.c, here.b].reshape(640, 256), grad[0])
    for k in range(1, 8):
        part = part + dot(hx[k - 1].reshape(640, 256), grad[k])
    acc[...] = part
    for j in range(1, 8):
        net.got(r3.at[j], s2_sem.at[j])
        prompt = prompt + r3[j].astype(F32)
    pg_ref[...] = prompt.astype(BF16)
    gp[0, 64:] = prompt.astype(BF16)
    share(prompt_part, prompt_part, gp_sem)

    query_part(3)
    query_part(4)
    part = acc[...] + dot(ht[here.c, here.b, :, :, :, HD:].reshape(640, HD), gp[0])
    for k in range(1, 8):
        net.got(prompt_part(k), gp_sem.at[k])
        part = part + dot(hx[k - 1, :, :, :, HD:].reshape(640, HD), gp[k])
    acc[...] = part
    wpart[...] = part.astype(BF16).reshape(2, 4, 80, 256)
    for j in range(1, 8):
        s = lax.rem(here.s + j, 8)
        net.push(wpart.at[lax.rem(s, 2), s // 2], wr3.at[8 - j], w_sem.at[8 - j], here.near(j))
    query_part(5)
    stores = []
    for h in range(HEADS):
        rows, cols = pl.ds(h * ROLL, ROLL), pl.ds(h * HD, HD)
        copy = pltpu.make_async_copy(dq.at[rows], dq_ref.at[:, cols], local.at[len(loads) + h])
        copy.start()
        stores.append(copy)
    total = acc[pl.ds(pl.multiple_of((here.z * 4 + here.a) * 80, 80), 80), :]
    for j in range(1, 8):
        net.got(wr3.at[j], w_sem.at[j])
        total = total + wr3[j].astype(F32)
    wg[0] = total.astype(BF16)
    for j in range(1, 4):
        net.push(wg.at[0], wg.at[4 - j], wg_sem.at[4 - j], here.group(j))
    for j in range(1, 4):
        net.got(wg.at[j], wg_sem.at[j])
        total = total + wg[j].astype(F32)
    w_ref[...] = total
    for copy in stores:
        copy.wait()
    net.drain()


def whole(lengths, q, g, rc, cache, hr, hp):
    vmem, hbm = pl.BlockSpec(memory_space=pltpu.VMEM), pl.BlockSpec(memory_space=pl.ANY)
    dma = pltpu.SemaphoreType.DMA

    def buf(*shape, kind=BF16):
        return pltpu.VMEM(shape, kind)

    scratch = [
        buf(ROWS, HD), buf(ROWS, HD), buf(ROLL, 2 * HD), buf(256, 5120),
        buf(64, 64, 256), buf(HD, KEYS),
        buf(KEYS + ROLL, TILE, kind=F32), buf(KEYS + ROLL, TILE, kind=F32),
        buf(KEYS + ROLL, ROWS), buf(KEYS + ROLL, ROWS),
        buf(ROWS, HD),
        buf(2, 4, 2, 4, 80, 256), buf(7, 2, 4, 80, 256), buf(8, 256, 256), buf(8, 128, 256),
        buf(640, 256, kind=F32), buf(2, 4, 80, 256),
        buf(256, 2048), buf(256, 256), buf(256, 256), buf(8, 64, 256),
        buf(8, 80, 256), buf(4, 80, 256),
        dma((28,)), dma((SENDS,)), dma((32,)), dma((32,)), dma((8,)), dma((8,)), dma((8,)),
        dma((4,)), dma((6,)), dma((8,)), dma((8,)), dma((4,)),
    ]
    return pl.pallas_call(
        kernel,
        out_shape=(
            jax.ShapeDtypeStruct((ROLL, HEADS * HD), BF16),
            jax.ShapeDtypeStruct((ROLL, 2 * HD), BF16),
            jax.ShapeDtypeStruct((64, 2 * HD), BF16),
            jax.ShapeDtypeStruct((80, 2 * HD), F32),
        ),
        in_specs=[pl.BlockSpec(memory_space=pltpu.SMEM)] + [hbm] * 6,
        out_specs=(hbm, vmem, vmem, vmem),
        scratch_shapes=scratch,
        compiler_params=pltpu.CompilerParams(
            collective_id=0, has_side_effects=True, vmem_limit_bytes=63 << 20
        ),
    )(lengths, q, g, rc, cache, hr, hp)


def finish_kernel(*refs):
    ins, outs, bufs, sems = refs[:4], refs[4:8], refs[8:12], refs[12]
    into = [pltpu.make_async_copy(a, b, sems.at[i]) for i, (a, b) in enumerate(zip(ins, bufs))]
    out = [pltpu.make_async_copy(b, o, sems.at[4 + i]) for i, (b, o) in enumerate(zip(bufs, outs))]
    for copy in into:
        copy.start()
    for first, second in zip(into, out):
        first.wait()
        second.start()
    for copy in out:
        copy.wait()


def finish(arrays):
    hbm = pl.BlockSpec(memory_space=pl.ANY)
    return pl.pallas_call(
        finish_kernel,
        out_shape=tuple(jax.ShapeDtypeStruct(a.shape, a.dtype) for a in arrays),
        in_specs=[hbm] * 4,
        out_specs=(hbm,) * 4,
        scratch_shapes=[pltpu.VMEM(a.shape, a.dtype) for a in arrays] + [pltpu.SemaphoreType.DMA((8,))],
    )(*arrays)


def body(queries, grad_out, rollout_cache, prompt_cache, rollout_hidden, prompt_hidden, lengths):
    outs = whole(
        lengths, queries[0], grad_out[0], rollout_cache[0], prompt_cache[0], rollout_hidden[0], prompt_hidden[0]
    )
    dq, dr, pg, w = finish(outs)
    return (dq[None], dr[None], pg[None], w)


def solution(mesh):
    rows = P("grp", "ctx", None)
    in_specs = (rows,) * 6 + (P("grp", "ctx"),)
    out_specs = (rows, rows, rows, P("ctx", None))
    return jax.shard_map(body, mesh=mesh, in_specs=in_specs, out_specs=out_specs, check_vma=False)
```

```python
import functools
import math

import jax
import jax.numpy as jnp
from jax import lax
from jax.experimental import pallas as pl
from jax.experimental.pallas import tpu as pltpu
from jax.sharding import PartitionSpec as P

MESH = pl.DeviceIdType.MESH
F32, BF16 = jnp.float32, jnp.bfloat16
KEYS, ROLL, ROWS, HD, HEADS = 4096, 192, 1536, 128, 8
CHUNK, TILE = 256, 256
SCALE = 1.0 / math.sqrt(HD)
EXP_SCALE = math.log2(math.e) * SCALE


def dot(a, b):
    return jnp.dot(a, b, preferred_element_type=F32)


def dot_nt(a, b):
    return lax.dot_general(a, b, (((1,), (1,)), ((), ())), preferred_element_type=F32)


class Place:
    def __init__(self):
        self.g = lax.axis_index("grp")
        t = lax.axis_index("ctx")
        self.t = t
        self.c = lax.rem(t, 2)
        y = lax.rem(t // 2, 4)
        x = lax.rem(t // 8, 4)
        self.z = t // 32
        self.a = x + self.c * (y - x)
        self.b = y + self.c * (x - y)
        self.s = self.a * 2 + self.z

    def dev(self, a, b, z, core):
        x = a + self.c * (b - a)
        y = b + self.c * (a - b)
        return (self.g, z * 32 + x * 8 + y * 2 + core)

    def ring(self, i):
        return self.dev(self.a, lax.rem(self.b + i, 4), self.z, self.c)

    def near(self, j):
        s = lax.rem(self.s + j, 8)
        return self.dev(s // 2, self.b, lax.rem(s, 2), self.c)

    def cross_a(self, i):
        return self.dev(lax.rem(self.a + i, 4), self.b, self.z, 1 - self.c)

    def cross_b(self, i):
        return self.dev(self.a, lax.rem(self.b + i, 4), self.z, 1 - self.c)

    def group(self, j):
        return (lax.rem(self.g + j, 4), self.t)

    def partners(self):
        ring = [self.ring(i) for i in range(1, 4)]
        near = [self.near(j) for j in range(1, 8)]
        cross = [self.cross_a(i) for i in range(4)] + [self.cross_b(i) for i in range(1, 4)]
        return ring + near + cross + [self.group(j) for j in range(1, 4)]


def greet(devices):
    for device in devices:
        pl.semaphore_signal(pltpu.get_barrier_semaphore(), inc=1, device_id=device, device_id_type=MESH)


class Net:
    def __init__(self, send, here):
        self.send, self.here, self.copies = send, here, []

    def copy(self, src, dst, sem, recv, device):
        return pltpu.make_async_remote_copy(
            src_ref=src, dst_ref=dst, send_sem=sem, recv_sem=recv, device_id=device, device_id_type=MESH
        )

    def push(self, src, dst, recv, device):
        copy = self.copy(src, dst, self.send.at[len(self.copies)], recv, device)
        copy.start()
        self.copies.append(copy)

    def got(self, dst, recv):
        self.copy(dst, dst, self.send.at[0], recv, self.here.cross_a(0)).wait_recv()

    def drain(self):
        for copy in self.copies:
            copy.wait_send()


SENDS = 63 + 7 + 7 + 14 + 10 + 14 + 14 + 6
FAR_FIRST = (5, 3, 7, 1, 4, 2, 6)
SOON_FIRST = (0, 2, 6, 4, 1, 7, 3, 5)


def kernel(
    len_ref, q_ref, g_ref, rc_ref, cache_ref, hr_ref, hp_ref,
    dq_ref, dr_ref, pg_ref, w_ref,
    qa, ga, rc, hbuf, kv, kt, E, DP, PB, DS, ht, hx, grad, gp, acc, wpart,
    r0, ra, rb, r3, wr3, wg,
    local, send, near_sem, core_sem, h_sem, gr_sem, gp_sem, s0_sem, s1_sem, s2_sem, w_sem, wg_sem,
):
    here = Place()
    net = Net(send, here)
    dq = qa
    dp, r2a, r2b = hbuf, hbuf.at[:, pl.ds(KEYS, 512)], hbuf.at[:, pl.ds(KEYS + 512, 512)]
    loads = []

    def load(src, dst):
        copy = pltpu.make_async_copy(src, dst, local.at[len(loads)])
        copy.start()
        loads.append(copy)

    load(cache_ref, kv.at[0])
    load(hr_ref, hbuf.at[pl.ds(0, ROLL)])
    load(hp_ref, hbuf.at[pl.ds(ROLL, 64)])
    load(rc_ref, rc)
    for h in range(HEADS):
        rows, cols = pl.ds(h * ROLL, ROLL), pl.ds(h * HD, HD)
        load(q_ref.at[:, cols], qa.at[rows])
        load(g_ref.at[:, cols], ga.at[rows])
    partners = here.partners()
    greet(partners)

    grad[:, ROLL:] = jnp.zeros((8, 64, 256), BF16)
    gp[:, :64] = jnp.zeros((8, 64, 256), BF16)
    loads[1].wait()
    loads[2].wait()
    for k in range(8):
        z, x = k // 4, k % 4
        part = hbuf[:, k * 640 : (k + 1) * 640].T.reshape(4, 2, 80, 256)
        for y in range(4):
            ht[0, y, z, x] = part[y, 0]
            ht[1, x, z, y] = part[y, 1]
    pl.semaphore_wait(pltpu.get_barrier_semaphore(), len(partners))

    loads[0].wait()
    core = here.cross_a(0)
    up, down = here.ring(1), here.ring(3)
    for j in FAR_FIRST:
        net.push(kv.at[0], kv.at[8 - j], near_sem.at[8 - j], here.near(j))

    def spread(j):
        net.push(kv.at[j], kv.at[24 + j], near_sem.at[24 + j], up)
        net.push(kv.at[j], kv.at[8 + j], near_sem.at[8 + j], down)
        net.push(kv.at[j], kv.at[32 + j], core_sem.at[j], core)

    def arrived(k):
        net.got(kv.at[k], near_sem.at[k])

    def to_core(k):
        net.push(kv.at[k], kv.at[32 + k], core_sem.at[k], core)

    spread(0)
    for j in SOON_FIRST[1:]:
        arrived(j)
        spread(j)

    def pass_on():
        for i, k in enumerate(SOON_FIRST):
            arrived(24 + k)
            if i < 4:
                net.push(kv.at[24 + k], kv.at[16 + k], near_sem.at[16 + k], up)
            to_core(24 + k)
            arrived(8 + k)
            if i >= 4:
                net.push(kv.at[8 + k], kv.at[16 + k], near_sem.at[16 + k], down)
            to_core(8 + k)

    def pass_last():
        for k in SOON_FIRST:
            arrived(16 + k)
            to_core(16 + k)
        for i in range(1, 4):
            net.push(ht.at[here.c, lax.rem(here.b + i, 4)], hx.at[3 - i], h_sem.at[4 - i], here.ring(i))
        for i in range(4):
            slot = 4 + (4 - i) % 4
            net.push(ht.at[1 - here.c, lax.rem(here.a + i, 4)], hx.at[slot - 1], h_sem.at[slot], here.cross_a(i))

    def from_core(b):
        for k in range(8 * b, 8 * b + 8):
            net.got(kv.at[32 + k], core_sem.at[k])

    for copy in loads[3:]:
        copy.wait()

    def keys(at, size):
        return kv[at // 64 : (at + size) // 64, :, :HD].reshape(size, HD)

    def values(at, size):
        return kv[at // 64 : (at + size) // 64, :, HD:].reshape(size, HD)

    roll_kt = rc[:, :HD].T
    n0, n1 = len_ref[0, 0], len_ref[0, 1]
    parts = [(KEYS, ROLL)]
    for b in (0, 3, 1, 2, 4, 7, 5, 6):
        parts += [(b * 512, CHUNK), (b * 512 + CHUNK, CHUNK)]
    due = {3 * 512: pass_on, 2 * 512: pass_last}
    due.update({(4 + b) * 512: functools.partial(from_core, b) for b in range(4)})
    for r0_ in range(0, ROWS, TILE):
        q, g = qa[r0_ : r0_ + TILE, :], ga[r0_ : r0_ + TILE, :]
        rows = lax.broadcasted_iota(jnp.int32, (1, TILE), 1) + r0_
        w = lax.rem(rows, ROLL)
        row_slot = (w >= 96).astype(jnp.int32)
        t = w - 96 * row_slot
        lim = jnp.where(row_slot == 1, n1, n0)
        live = (t < lim).astype(F32)
        idx = lax.broadcasted_iota(jnp.int32, (ROLL, 1), 0)
        key_slot = (idx >= 96).astype(jnp.int32)
        u = idx - 96 * key_slot
        ok = (key_slot == row_slot) & (u <= t) & (u < lim)
        top = jnp.full((8, TILE), -1e30, F32)
        total = jnp.zeros((8, TILE), F32)
        weighted = jnp.zeros((8, TILE), F32)
        tops = []
        for at, n in parts:
            if r0_ == 0 and at in due:
                due[at]()
            if at < KEYS:
                s = dot_nt(keys(at, n), q) * EXP_SCALE
                d = dot_nt(values(at, n), g)
            else:
                s = jnp.where(ok, dot_nt(rc[:, :HD], q) * EXP_SCALE, -1e30)
                d = dot_nt(rc[:, HD:], g)
            s = s.reshape(n // 8, 8, TILE)
            newest = jnp.maximum(top, jnp.max(s, axis=0))
            shrink = jnp.exp2(top - newest)
            top = newest
            e = jnp.exp2(s - top[None])
            E[at : at + n, :] = e.reshape(n, TILE)
            DP[at : at + n, :] = d
            total = total * shrink + jnp.sum(e, axis=0)
            weighted = weighted * shrink + jnp.sum(e * d.reshape(n // 8, 8, TILE), axis=0)
            tops.append(top)
        highest = jnp.max(top, axis=0, keepdims=True)
        last = jnp.exp2(top - highest)
        sums = jnp.sum(total * last, axis=0, keepdims=True)
        delta = jnp.broadcast_to(jnp.sum(weighted * last, axis=0, keepdims=True) / sums, (8, TILE))
        inv = live / sums
        for (at, n), old in zip(parts, tops):
            factor = jnp.exp2(old - highest) * inv
            p = E[at : at + n, :].reshape(n // 8, 8, TILE) * factor[None]
            ds = (p * (DP[at : at + n, :].reshape(n // 8, 8, TILE) - delta[None])).reshape(n, TILE).astype(BF16)
            PB[at : at + n, r0_ : r0_ + TILE] = p.reshape(n, TILE).astype(BF16)
            DS[at : at + n, r0_ : r0_ + TILE] = ds

    for c in range(8):
        kt[:, c * 512 : (c + 1) * 512] = keys(c * 512, 512).T

    def query_part(i):
        cols = slice(i * TILE, (i + 1) * TILE)
        turned = dot(kt[...], DS[:KEYS, cols]) + dot(roll_kt, DS[KEYS:, cols])
        dq[cols, :] = (turned.T * SCALE).astype(BF16)

    def grads(at, n):
        both = [dot(DS[at : at + n, :], qa[...]) * SCALE, dot(PB[at : at + n, :], ga[...])]
        return jnp.concatenate(both, axis=1).astype(BF16)

    def share(part, sems, first):
        for i in (2, 1, 3):
            net.push(part(0), part(4 - i), sems.at[first + 4 - i], here.ring(i))
        for i in (2, 1, 3, 0):
            slot = 4 + (4 - i) % 4
            net.push(part(0), part(slot), sems.at[first + slot], here.cross_a(i))

    def half(h):
        return pl.ds(h * HD, HD)

    def roll_part(k):
        return grad.at[k, pl.ds(0, ROLL)]

    def prompt_part(h, k):
        return gp.at[k, pl.ds(64, 64), half(h)]

    mine = grads(KEYS, ROLL)
    dr_ref[...] = mine
    grad[0, :ROLL] = mine

    def cell(ref, k):
        return ref.at[pl.ds(k % 4 * 64, 64), pl.ds(k // 4 * 256, 256)]

    def cells(ref, k, n):
        return ref.at[:, pl.ds(k // 4 * 256, n // 4 * 256)]

    def block(k):
        new = grads(k * 512, 512)
        cells(dp, k * 8, 4)[...] = new[:256]
        cells(dp, k * 8 + 4, 4)[...] = new[256:]

    def other(b):
        block(4 + b)
        net.push(cells(dp, 32 + b * 8, 8), cells(r0, b * 8, 8), s0_sem.at[b], core)

    def merge(at, n, extra=None):
        total = cells(dp, at, n)[...].astype(F32) + cells(r0, at, n)[...].astype(F32)
        if extra is not None:
            total = total + extra[...].astype(F32)
        cells(r0, at, n)[...] = total.astype(BF16)

    def got_core(b):
        net.got(cells(r0, b * 8, 8), s0_sem.at[b])

    other(2)
    block(2)
    other(1)
    got_core(2)
    merge(16, 8)
    net.push(cells(r0, 16, 4), ra, s1_sem.at[0], up)
    net.push(cells(r0, 20, 4), rb, s1_sem.at[1], down)
    other(3)
    block(1)
    got_core(1)
    merge(12, 4)
    net.push(cells(r0, 12, 4), cells(r2a, 4, 4), s1_sem.at[2], up)
    block(3)
    got_core(3)
    merge(24, 4)
    net.push(cells(r0, 24, 4), cells(r2b, 0, 4), s1_sem.at[3], down)
    other(0)
    net.got(ra, s1_sem.at[0])
    merge(8, 4, ra)
    net.push(cells(r0, 8, 4), cells(r2a, 0, 4), s1_sem.at[4], up)
    net.got(rb, s1_sem.at[1])
    merge(28, 4, rb)
    net.push(cells(r0, 28, 4), cells(r2b, 4, 4), s1_sem.at[5], down)
    block(0)
    query_part(0)
    got_core(0)
    net.got(cells(r2a, 4, 4), s1_sem.at[2])
    net.got(cells(r2b, 0, 4), s1_sem.at[3])
    net.got(cells(r2a, 0, 4), s1_sem.at[4])
    net.got(cells(r2b, 4, 4), s1_sem.at[5])

    def own(k):
        return sum(cell(ref, k)[...].astype(F32) for ref in (dp, r0, r2a, r2b))

    for j in range(1, 8):
        cell(r0, j)[...] = own(j).astype(BF16)
    for h in (1, 0):
        for j in FAR_FIRST:
            net.push(cell(r0, j).at[:, half(h)], r3.at[7 - j, :, half(h)], s2_sem.at[h * 8 + 8 - j], here.near(j))
    share(roll_part, gr_sem, 0)
    prompt = own(0)
    query_part(1)
    query_part(2)
    query_part(3)
    for h in (1, 0):
        total = prompt[:, h * HD : (h + 1) * HD]
        for j in SOON_FIRST[1:]:
            net.got(r3.at[j - 1, :, half(h)], s2_sem.at[h * 8 + j])
            total = total + r3[j - 1, :, half(h)].astype(F32)
        pg_ref[:, half(h)] = total.astype(BF16)
        prompt_part(h, 0)[...] = total.astype(BF16)
        share(functools.partial(prompt_part, h), gp_sem, h * 8)

    part = dot(ht[here.c, here.b].reshape(640, 256), grad[0])
    for k in range(1, 8):
        net.got(hx.at[k - 1], h_sem.at[k])
        net.got(roll_part(k), gr_sem.at[k])
        part = part + dot(hx[k - 1].reshape(640, 256), grad[k])
    acc[...] = part
    query_part(4)
    for h in (1, 0):
        part = acc[:, half(h)] + dot(ht[here.c, here.b, :, :, :, HD:].reshape(640, HD), gp[0, :, half(h)])
        for k in range(1, 8):
            net.got(prompt_part(h, k), gp_sem.at[h * 8 + k])
            part = part + dot(hx[k - 1, :, :, :, HD:].reshape(640, HD), gp[k, :, half(h)])
        acc[:, half(h)] = part
        wpart[:, :, :, half(h)] = part.astype(BF16).reshape(2, 4, 80, HD)
        for j in FAR_FIRST:
            s = lax.rem(here.s + j, 8)
            src = wpart.at[lax.rem(s, 2), s // 2, :, half(h)]
            net.push(src, wr3.at[7 - j, :, half(h)], w_sem.at[h * 8 + 8 - j], here.near(j))
    query_part(5)
    stores = []
    for h in range(HEADS):
        rows, cols = pl.ds(h * ROLL, ROLL), pl.ds(h * HD, HD)
        copy = pltpu.make_async_copy(dq.at[rows], dq_ref.at[:, cols], local.at[len(loads) + h])
        copy.start()
        stores.append(copy)
    totals = {}
    for h in (1, 0):
        total = acc[pl.ds(pl.multiple_of((here.z * 4 + here.a) * 80, 80), 80), half(h)]
        for j in SOON_FIRST[1:]:
            net.got(wr3.at[j - 1, :, half(h)], w_sem.at[h * 8 + j])
            total = total + wr3[j - 1, :, half(h)].astype(F32)
        wg[0, :, half(h)] = total.astype(BF16)
        for j in (2, 1, 3):
            net.push(wg.at[0, :, half(h)], wg.at[4 - j, :, half(h)], wg_sem.at[h * 4 + 4 - j], here.group(j))
        totals[h] = total
    for h in (1, 0):
        total = totals[h]
        for j in (1, 3, 2):
            net.got(wg.at[j, :, half(h)], wg_sem.at[h * 4 + j])
            total = total + wg[j, :, half(h)].astype(F32)
        w_ref[:, half(h)] = total
    for copy in stores:
        copy.wait()
    net.drain()


def whole(lengths, q, g, rc, cache, hr, hp):
    vmem, hbm = pl.BlockSpec(memory_space=pltpu.VMEM), pl.BlockSpec(memory_space=pl.ANY)
    dma = pltpu.SemaphoreType.DMA

    def buf(*shape, kind=BF16):
        return pltpu.VMEM(shape, kind)

    scratch = [
        buf(ROWS, HD), buf(ROWS, HD), buf(ROLL, 2 * HD), buf(256, 5120),
        buf(64, 64, 256), buf(HD, KEYS),
        buf(KEYS + ROLL, TILE, kind=F32), buf(KEYS + ROLL, TILE, kind=F32),
        buf(KEYS + ROLL, ROWS), buf(KEYS + ROLL, ROWS),
        buf(2, 4, 2, 4, 80, 256), buf(7, 2, 4, 80, 256), buf(8, 256, 256), buf(8, 128, 256),
        buf(640, 256, kind=F32), buf(2, 4, 80, 256),
        buf(256, 2048), buf(256, 256), buf(256, 256), buf(7, 64, 256),
        buf(7, 80, 256), buf(4, 80, 256),
        dma((28,)), dma((SENDS,)), dma((32,)), dma((32,)), dma((8,)), dma((8,)), dma((16,)),
        dma((4,)), dma((6,)), dma((16,)), dma((16,)), dma((8,)),
    ]
    return pl.pallas_call(
        kernel,
        out_shape=(
            jax.ShapeDtypeStruct((ROLL, HEADS * HD), BF16),
            jax.ShapeDtypeStruct((ROLL, 2 * HD), BF16),
            jax.ShapeDtypeStruct((64, 2 * HD), BF16),
            jax.ShapeDtypeStruct((80, 2 * HD), F32),
        ),
        in_specs=[pl.BlockSpec(memory_space=pltpu.SMEM)] + [hbm] * 6,
        out_specs=(hbm, vmem, vmem, vmem),
        scratch_shapes=scratch,
        compiler_params=pltpu.CompilerParams(
            collective_id=0, has_side_effects=True, vmem_limit_bytes=(63 << 20) + (512 << 10)
        ),
    )(lengths, q, g, rc, cache, hr, hp)


def finish_kernel(*refs):
    ins, outs, bufs, sems = refs[:4], refs[4:8], refs[8:12], refs[12]
    into = [pltpu.make_async_copy(a, b, sems.at[i]) for i, (a, b) in enumerate(zip(ins, bufs))]
    out = [pltpu.make_async_copy(b, o, sems.at[4 + i]) for i, (b, o) in enumerate(zip(bufs, outs))]
    for copy in into:
        copy.start()
    for first, second in zip(into, out):
        first.wait()
        second.start()
    for copy in out:
        copy.wait()


def finish(arrays):
    hbm = pl.BlockSpec(memory_space=pl.ANY)
    return pl.pallas_call(
        finish_kernel,
        out_shape=tuple(jax.ShapeDtypeStruct(a.shape, a.dtype) for a in arrays),
        in_specs=[hbm] * 4,
        out_specs=(hbm,) * 4,
        scratch_shapes=[pltpu.VMEM(a.shape, a.dtype) for a in arrays] + [pltpu.SemaphoreType.DMA((8,))],
    )(*arrays)


def body(queries, grad_out, rollout_cache, prompt_cache, rollout_hidden, prompt_hidden, lengths):
    outs = whole(
        lengths, queries[0], grad_out[0], rollout_cache[0], prompt_cache[0], rollout_hidden[0], prompt_hidden[0]
    )
    dq, dr, pg, w = finish(outs)
    return (dq[None], dr[None], pg[None], w)


def solution(mesh):
    rows = P("grp", "ctx", None)
    in_specs = (rows,) * 6 + (P("grp", "ctx"),)
    out_specs = (rows, rows, rows, P("ctx", None))
    return jax.shard_map(body, mesh=mesh, in_specs=in_specs, out_specs=out_specs, check_vma=False)
```

```python
import functools
import math

import jax
import jax.numpy as jnp
from jax import lax
from jax.experimental import pallas as pl
from jax.experimental.pallas import tpu as pltpu
from jax.sharding import PartitionSpec as P

MESH = pl.DeviceIdType.MESH
F32, BF16 = jnp.float32, jnp.bfloat16
KEYS, ROLL, ROWS, HD, HEADS = 4096, 192, 1536, 128, 8
CHUNK, TILE = 256, 256
SCALE = 1.0 / math.sqrt(HD)
EXP_SCALE = math.log2(math.e) * SCALE


def dot(a, b):
    return jnp.dot(a, b, preferred_element_type=F32)


def dot_nt(a, b):
    return lax.dot_general(a, b, (((1,), (1,)), ((), ())), preferred_element_type=F32)


class Place:
    def __init__(self):
        self.g = lax.axis_index("grp")
        t = lax.axis_index("ctx")
        self.t = t
        self.c = lax.rem(t, 2)
        y = lax.rem(t // 2, 4)
        x = lax.rem(t // 8, 4)
        self.z = t // 32
        self.a = x + self.c * (y - x)
        self.b = y + self.c * (x - y)
        self.s = self.a * 2 + self.z

    def dev(self, a, b, z, core):
        x = a + self.c * (b - a)
        y = b + self.c * (a - b)
        return (self.g, z * 32 + x * 8 + y * 2 + core)

    def ring(self, i):
        return self.dev(self.a, lax.rem(self.b + i, 4), self.z, self.c)

    def near(self, j):
        s = lax.rem(self.s + j, 8)
        return self.dev(s // 2, self.b, lax.rem(s, 2), self.c)

    def cross_a(self, i):
        return self.dev(lax.rem(self.a + i, 4), self.b, self.z, 1 - self.c)

    def cross_b(self, i):
        return self.dev(self.a, lax.rem(self.b + i, 4), self.z, 1 - self.c)

    def group(self, j):
        return (lax.rem(self.g + j, 4), self.t)

    def partners(self):
        ring = [self.ring(i) for i in range(1, 4)]
        near = [self.near(j) for j in range(1, 8)]
        cross = [self.cross_a(i) for i in range(4)] + [self.cross_b(i) for i in range(1, 4)]
        return ring + near + cross + [self.group(j) for j in range(1, 4)]


def greet(devices):
    for device in devices:
        pl.semaphore_signal(pltpu.get_barrier_semaphore(), inc=1, device_id=device, device_id_type=MESH)


class Net:
    def __init__(self, send, here):
        self.send, self.here, self.copies = send, here, []

    def copy(self, src, dst, sem, recv, device):
        return pltpu.make_async_remote_copy(
            src_ref=src, dst_ref=dst, send_sem=sem, recv_sem=recv, device_id=device, device_id_type=MESH
        )

    def push(self, src, dst, recv, device):
        copy = self.copy(src, dst, self.send.at[len(self.copies)], recv, device)
        copy.start()
        self.copies.append(copy)

    def got(self, dst, recv):
        self.copy(dst, dst, self.send.at[0], recv, self.here.cross_a(0)).wait_recv()

    def drain(self):
        for copy in self.copies:
            copy.wait_send()


SENDS = 63 + 7 + 7 + 14 + 10 + 14 + 14 + 6
FAR_FIRST = (5, 3, 7, 1, 4, 2, 6)
SOON_FIRST = (0, 2, 6, 4, 1, 7, 3, 5)


def kernel(
    len_ref, q_ref, g_ref, rc_ref, cache_ref, hr_ref, hp_ref,
    dq_ref, dr_ref, pg_ref, w_ref,
    qa, ga, rc, hbuf, kv, kt, E, DP, PB, DS, ht, hx, grad, gp, acc, wpart,
    r0, ra, rb, r3, wr3, wg,
    local, send, near_sem, core_sem, h_sem, gr_sem, gp_sem, s0_sem, s1_sem, s2_sem, w_sem, wg_sem,
):
    here = Place()
    net = Net(send, here)
    dq = qa
    dp, r2a, r2b = hbuf, hbuf.at[:, pl.ds(KEYS, 512)], hbuf.at[:, pl.ds(KEYS + 512, 512)]
    loads = []

    def load(src, dst):
        copy = pltpu.make_async_copy(src, dst, local.at[len(loads)])
        copy.start()
        loads.append(copy)

    load(cache_ref, kv.at[0])
    load(hr_ref, hbuf.at[pl.ds(0, ROLL)])
    load(hp_ref, hbuf.at[pl.ds(ROLL, 64)])
    load(rc_ref, rc)
    for h in range(HEADS):
        rows, cols = pl.ds(h * ROLL, ROLL), pl.ds(h * HD, HD)
        load(q_ref.at[:, cols], qa.at[rows])
        load(g_ref.at[:, cols], ga.at[rows])
    partners = here.partners()
    greet(partners)

    grad[:, ROLL:] = jnp.zeros((8, 64, 256), BF16)
    gp[:, :64] = jnp.zeros((8, 64, 256), BF16)
    loads[1].wait()
    loads[2].wait()
    for k in range(8):
        z, x = k // 4, k % 4
        part = hbuf[:, k * 640 : (k + 1) * 640].T.reshape(4, 2, 80, 256)
        for y in range(4):
            ht[0, y, z, x] = part[y, 0]
            ht[1, x, z, y] = part[y, 1]
    pl.semaphore_wait(pltpu.get_barrier_semaphore(), len(partners))

    loads[0].wait()
    core = here.cross_a(0)
    up, down = here.ring(1), here.ring(3)
    for j in FAR_FIRST:
        net.push(kv.at[0], kv.at[8 - j], near_sem.at[8 - j], here.near(j))

    def spread(j):
        net.push(kv.at[j], kv.at[24 + j], near_sem.at[24 + j], up)
        net.push(kv.at[j], kv.at[8 + j], near_sem.at[8 + j], down)
        net.push(kv.at[j], kv.at[32 + j], core_sem.at[j], core)

    def arrived(k):
        net.got(kv.at[k], near_sem.at[k])

    def to_core(k):
        net.push(kv.at[k], kv.at[32 + k], core_sem.at[k], core)

    spread(0)
    for j in SOON_FIRST[1:]:
        arrived(j)
        spread(j)

    def pass_on():
        for i, k in enumerate(SOON_FIRST):
            arrived(24 + k)
            if i < 4:
                net.push(kv.at[24 + k], kv.at[16 + k], near_sem.at[16 + k], up)
            to_core(24 + k)
            arrived(8 + k)
            if i >= 4:
                net.push(kv.at[8 + k], kv.at[16 + k], near_sem.at[16 + k], down)
            to_core(8 + k)

    def pass_last():
        for k in SOON_FIRST:
            arrived(16 + k)
            to_core(16 + k)
        for i in range(1, 4):
            net.push(ht.at[here.c, lax.rem(here.b + i, 4)], hx.at[3 - i], h_sem.at[4 - i], here.ring(i))
        for i in range(4):
            slot = 4 + (4 - i) % 4
            net.push(ht.at[1 - here.c, lax.rem(here.a + i, 4)], hx.at[slot - 1], h_sem.at[slot], here.cross_a(i))

    def from_core(b):
        for k in range(8 * b, 8 * b + 8):
            net.got(kv.at[32 + k], core_sem.at[k])

    for copy in loads[3:]:
        copy.wait()

    def keys(at, size):
        return kv[at // 64 : (at + size) // 64, :, :HD].reshape(size, HD)

    def values(at, size):
        return kv[at // 64 : (at + size) // 64, :, HD:].reshape(size, HD)

    roll_kt = rc[:, :HD].T
    n0, n1 = len_ref[0, 0], len_ref[0, 1]
    parts = [(KEYS, ROLL)]
    for b in (0, 3, 1, 2, 4, 7, 5, 6):
        parts += [(b * 512, CHUNK), (b * 512 + CHUNK, CHUNK)]
    due = {3 * 512: pass_on, 2 * 512: pass_last}
    due.update({(4 + b) * 512: functools.partial(from_core, b) for b in range(4)})
    for r0_ in range(0, ROWS, TILE):
        q, g = qa[r0_ : r0_ + TILE, :], ga[r0_ : r0_ + TILE, :]
        rows = lax.broadcasted_iota(jnp.int32, (1, TILE), 1) + r0_
        w = lax.rem(rows, ROLL)
        row_slot = (w >= 96).astype(jnp.int32)
        t = w - 96 * row_slot
        lim = jnp.where(row_slot == 1, n1, n0)
        live = (t < lim).astype(F32)
        idx = lax.broadcasted_iota(jnp.int32, (ROLL, 1), 0)
        key_slot = (idx >= 96).astype(jnp.int32)
        u = idx - 96 * key_slot
        ok = (key_slot == row_slot) & (u <= t) & (u < lim)
        top = jnp.full((8, TILE), -1e30, F32)
        total = jnp.zeros((8, TILE), F32)
        weighted = jnp.zeros((8, TILE), F32)
        tops = []
        for at, n in parts:
            if r0_ == 0 and at in due:
                due[at]()
            if at < KEYS:
                s = dot_nt(keys(at, n), q) * EXP_SCALE
                d = dot_nt(values(at, n), g)
            else:
                s = jnp.where(ok, dot_nt(rc[:, :HD], q) * EXP_SCALE, -1e30)
                d = dot_nt(rc[:, HD:], g)
            s = s.reshape(n // 8, 8, TILE)
            newest = jnp.maximum(top, jnp.max(s, axis=0))
            shrink = jnp.exp2(top - newest)
            top = newest
            e = jnp.exp2(s - top[None])
            E[at : at + n, :] = e.reshape(n, TILE)
            DP[at : at + n, :] = d
            total = total * shrink + jnp.sum(e, axis=0)
            weighted = weighted * shrink + jnp.sum(e * d.reshape(n // 8, 8, TILE), axis=0)
            tops.append(top)
        highest = jnp.max(top, axis=0, keepdims=True)
        last = jnp.exp2(top - highest)
        sums = jnp.sum(total * last, axis=0, keepdims=True)
        delta = jnp.broadcast_to(jnp.sum(weighted * last, axis=0, keepdims=True) / sums, (8, TILE))
        inv = live / sums
        for (at, n), old in zip(parts, tops):
            factor = jnp.exp2(old - highest) * inv
            p = E[at : at + n, :].reshape(n // 8, 8, TILE) * factor[None]
            ds = (p * (DP[at : at + n, :].reshape(n // 8, 8, TILE) - delta[None])).reshape(n, TILE).astype(BF16)
            PB[at : at + n, r0_ : r0_ + TILE] = p.reshape(n, TILE).astype(BF16)
            DS[at : at + n, r0_ : r0_ + TILE] = ds

    for c in range(8):
        kt[:, c * 512 : (c + 1) * 512] = keys(c * 512, 512).T

    def query_part(i):
        cols = slice(i * TILE, (i + 1) * TILE)
        turned = dot(kt[...], DS[:KEYS, cols]) + dot(roll_kt, DS[KEYS:, cols])
        dq[cols, :] = (turned.T * SCALE).astype(BF16)

    def grads(at, n):
        both = [dot(DS[at : at + n, :], qa[...]) * SCALE, dot(PB[at : at + n, :], ga[...])]
        return jnp.concatenate(both, axis=1).astype(BF16)

    def share(part, sems, first):
        for i in (2, 1, 3):
            net.push(part(0), part(4 - i), sems.at[first + 4 - i], here.ring(i))
        for i in (2, 1, 3, 0):
            slot = 4 + (4 - i) % 4
            net.push(part(0), part(slot), sems.at[first + slot], here.cross_a(i))

    def half(h):
        return pl.ds(h * HD, HD)

    def roll_part(k):
        return grad.at[k, pl.ds(0, ROLL)]

    def prompt_part(h, k):
        return gp.at[k, pl.ds(64, 64), half(h)]

    mine = grads(KEYS, ROLL)
    dr_ref[...] = mine
    grad[0, :ROLL] = mine

    def cell(ref, k):
        return ref.at[pl.ds(k % 4 * 64, 64), pl.ds(k // 4 * 256, 256)]

    def cells(ref, k, n):
        return ref.at[:, pl.ds(k // 4 * 256, n // 4 * 256)]

    def block(k):
        new = grads(k * 512, 512)
        cells(dp, k * 8, 4)[...] = new[:256]
        cells(dp, k * 8 + 4, 4)[...] = new[256:]

    def other(b):
        block(4 + b)
        net.push(cells(dp, 32 + b * 8, 8), cells(r0, b * 8, 8), s0_sem.at[b], core)

    def merge(at, n, extra=None):
        total = cells(dp, at, n)[...].astype(F32) + cells(r0, at, n)[...].astype(F32)
        if extra is not None:
            total = total + extra[...].astype(F32)
        cells(r0, at, n)[...] = total.astype(BF16)

    def got_core(b):
        net.got(cells(r0, b * 8, 8), s0_sem.at[b])

    other(2)
    block(2)
    other(1)
    got_core(2)
    merge(16, 8)
    net.push(cells(r0, 16, 4), ra, s1_sem.at[0], up)
    net.push(cells(r0, 20, 4), rb, s1_sem.at[1], down)
    other(3)
    block(1)
    got_core(1)
    merge(12, 4)
    net.push(cells(r0, 12, 4), cells(r2a, 4, 4), s1_sem.at[2], up)
    block(3)
    got_core(3)
    merge(24, 4)
    net.push(cells(r0, 24, 4), cells(r2b, 0, 4), s1_sem.at[3], down)
    other(0)
    net.got(ra, s1_sem.at[0])
    merge(8, 4, ra)
    net.push(cells(r0, 8, 4), cells(r2a, 0, 4), s1_sem.at[4], up)
    net.got(rb, s1_sem.at[1])
    merge(28, 4, rb)
    net.push(cells(r0, 28, 4), cells(r2b, 4, 4), s1_sem.at[5], down)
    block(0)
    query_part(0)
    got_core(0)
    net.got(cells(r2a, 4, 4), s1_sem.at[2])
    net.got(cells(r2b, 0, 4), s1_sem.at[3])
    net.got(cells(r2a, 0, 4), s1_sem.at[4])
    net.got(cells(r2b, 4, 4), s1_sem.at[5])

    def own(k):
        return sum(cell(ref, k)[...].astype(F32) for ref in (dp, r0, r2a, r2b))

    for j in range(1, 8):
        cell(r0, j)[...] = own(j).astype(BF16)
    for h in (1, 0):
        for j in FAR_FIRST:
            net.push(cell(r0, j).at[:, half(h)], r3.at[7 - j, :, half(h)], s2_sem.at[h * 8 + 8 - j], here.near(j))
    share(roll_part, gr_sem, 0)
    prompt = own(0)
    query_part(1)
    query_part(2)
    query_part(3)
    for h in (1, 0):
        total = prompt[:, h * HD : (h + 1) * HD]
        for j in SOON_FIRST[1:]:
            net.got(r3.at[j - 1, :, half(h)], s2_sem.at[h * 8 + j])
            total = total + r3[j - 1, :, half(h)].astype(F32)
        pg_ref[:, half(h)] = total.astype(BF16)
        prompt_part(h, 0)[...] = total.astype(BF16)
        share(functools.partial(prompt_part, h), gp_sem, h * 8)

    part = dot(ht[here.c, here.b].reshape(640, 256), grad[0])
    for k in range(1, 8):
        net.got(hx.at[k - 1], h_sem.at[k])
        net.got(roll_part(k), gr_sem.at[k])
        part = part + dot(hx[k - 1].reshape(640, 256), grad[k])
    acc[...] = part
    for h in (1, 0):
        part = acc[:, half(h)] + dot(ht[here.c, here.b, :, :, :, HD:].reshape(640, HD), gp[0, :, half(h)])
        for k in range(1, 8):
            net.got(prompt_part(h, k), gp_sem.at[h * 8 + k])
            part = part + dot(hx[k - 1, :, :, :, HD:].reshape(640, HD), gp[k, :, half(h)])
        acc[:, half(h)] = part
        wpart[:, :, :, half(h)] = part.astype(BF16).reshape(2, 4, 80, HD)
        for j in FAR_FIRST:
            s = lax.rem(here.s + j, 8)
            src = wpart.at[lax.rem(s, 2), s // 2, :, half(h)]
            net.push(src, wr3.at[7 - j, :, half(h)], w_sem.at[h * 8 + 8 - j], here.near(j))
    query_part(4)
    query_part(5)
    stores = []
    for h in range(HEADS):
        rows, cols = pl.ds(h * ROLL, ROLL), pl.ds(h * HD, HD)
        copy = pltpu.make_async_copy(dq.at[rows], dq_ref.at[:, cols], local.at[len(loads) + h])
        copy.start()
        stores.append(copy)
    totals = {}
    for h in (1, 0):
        total = acc[pl.ds(pl.multiple_of((here.z * 4 + here.a) * 80, 80), 80), half(h)]
        for j in SOON_FIRST[1:]:
            net.got(wr3.at[j - 1, :, half(h)], w_sem.at[h * 8 + j])
            total = total + wr3[j - 1, :, half(h)].astype(F32)
        wg[0, :, half(h)] = total.astype(BF16)
        for j in (2, 1, 3):
            net.push(wg.at[0, :, half(h)], wg.at[4 - j, :, half(h)], wg_sem.at[h * 4 + 4 - j], here.group(j))
        totals[h] = total
    for h in (1, 0):
        total = totals[h]
        for j in (1, 3, 2):
            net.got(wg.at[j, :, half(h)], wg_sem.at[h * 4 + j])
            total = total + wg[j, :, half(h)].astype(F32)
        w_ref[:, half(h)] = total
    for copy in stores:
        copy.wait()
    net.drain()


def whole(lengths, q, g, rc, cache, hr, hp):
    vmem, hbm = pl.BlockSpec(memory_space=pltpu.VMEM), pl.BlockSpec(memory_space=pl.ANY)
    dma = pltpu.SemaphoreType.DMA

    def buf(*shape, kind=BF16):
        return pltpu.VMEM(shape, kind)

    scratch = [
        buf(ROWS, HD), buf(ROWS, HD), buf(ROLL, 2 * HD), buf(256, 5120),
        buf(64, 64, 256), buf(HD, KEYS),
        buf(KEYS + ROLL, TILE, kind=F32), buf(KEYS + ROLL, TILE, kind=F32),
        buf(KEYS + ROLL, ROWS), buf(KEYS + ROLL, ROWS),
        buf(2, 4, 2, 4, 80, 256), buf(7, 2, 4, 80, 256), buf(8, 256, 256), buf(8, 128, 256),
        buf(640, 256, kind=F32), buf(2, 4, 80, 256),
        buf(256, 2048), buf(256, 256), buf(256, 256), buf(7, 64, 256),
        buf(7, 80, 256), buf(4, 80, 256),
        dma((28,)), dma((SENDS,)), dma((32,)), dma((32,)), dma((8,)), dma((8,)), dma((16,)),
        dma((4,)), dma((6,)), dma((16,)), dma((16,)), dma((8,)),
    ]
    return pl.pallas_call(
        kernel,
        out_shape=(
            jax.ShapeDtypeStruct((ROLL, HEADS * HD), BF16),
            jax.ShapeDtypeStruct((ROLL, 2 * HD), BF16),
            jax.ShapeDtypeStruct((64, 2 * HD), BF16),
            jax.ShapeDtypeStruct((80, 2 * HD), F32),
        ),
        in_specs=[pl.BlockSpec(memory_space=pltpu.SMEM)] + [hbm] * 6,
        out_specs=(hbm, vmem, vmem, vmem),
        scratch_shapes=scratch,
        compiler_params=pltpu.CompilerParams(
            collective_id=0, has_side_effects=True, vmem_limit_bytes=(63 << 20) + (512 << 10)
        ),
    )(lengths, q, g, rc, cache, hr, hp)


def finish_kernel(*refs):
    ins, outs, bufs, sems = refs[:4], refs[4:8], refs[8:12], refs[12]
    into = [pltpu.make_async_copy(a, b, sems.at[i]) for i, (a, b) in enumerate(zip(ins, bufs))]
    out = [pltpu.make_async_copy(b, o, sems.at[4 + i]) for i, (b, o) in enumerate(zip(bufs, outs))]
    for copy in into:
        copy.start()
    for first, second in zip(into, out):
        first.wait()
        second.start()
    for copy in out:
        copy.wait()


def finish(arrays):
    hbm = pl.BlockSpec(memory_space=pl.ANY)
    return pl.pallas_call(
        finish_kernel,
        out_shape=tuple(jax.ShapeDtypeStruct(a.shape, a.dtype) for a in arrays),
        in_specs=[hbm] * 4,
        out_specs=(hbm,) * 4,
        scratch_shapes=[pltpu.VMEM(a.shape, a.dtype) for a in arrays] + [pltpu.SemaphoreType.DMA((8,))],
    )(*arrays)


def body(queries, grad_out, rollout_cache, prompt_cache, rollout_hidden, prompt_hidden, lengths):
    outs = whole(
        lengths, queries[0], grad_out[0], rollout_cache[0], prompt_cache[0], rollout_hidden[0], prompt_hidden[0]
    )
    dq, dr, pg, w = finish(outs)
    return (dq[None], dr[None], pg[None], w)


def solution(mesh):
    rows = P("grp", "ctx", None)
    in_specs = (rows,) * 6 + (P("grp", "ctx"),)
    out_specs = (rows, rows, rows, P("ctx", None))
    return jax.shard_map(body, mesh=mesh, in_specs=in_specs, out_specs=out_specs, check_vma=False)
```
